32 devices in a mesh: layer: 4 (over y, core), grid: 8 (over z, x).
Axes of the slice: x: 2, y: 2, z: 4, core: 2. Of those that a mesh axis runs over, the one named last changes fastest.
Arguments:
- l_panels: bfloat16 [4, 2, 8192, 512], P('layer', None, 'grid'), may hold values from -6 to 6
- u_panels: bfloat16 [4, 2, 512, 512], P('layer', None, 'grid'), may hold values from -0.046875 to 0.046875
- panel_fill: int32 [4, 2, 64, 4], P('layer', None, 'grid'), may hold values 0 or 1
- copy_fill: int32 [4, 64, 4], P('layer', 'grid'), may hold values 0 or 1
- sep_panels: bfloat16 [3, 8192, 256], P(None, 'grid'), may hold values from -0.25 to 0.25
- sep_owner: int32 [3], replicated, may hold values from 0 to 7
Outputs:
- schur: float32 [8192, 512], P('grid', 'layer')
The draws below stay inside these ranges and needn't reach their ends.
All inputs are finite; a program needn't handle non-finite values. No bound on the sum of `panel_fill` or of `copy_fill` on one device may be relied on, other than what follows from the above.
Results may differ from the reference program's by a relative error of at most 0.0035.
Values may be sent and summed in bfloat16 or wider, within the bound.
No kernel may reach another device: no remote copies, remote signals or barrier semaphores. Data moves between devices by JAX's collectives and lax.ppermute only.
A program may use at most 64 MiB of HBM per device.

```python
import jax
import jax.numpy as jnp
from jax import lax

BLOCK = 128
S = 8192
W = 512
WS = 256
PANELS = 2
C = 512
NODES = 3
N_LAYER = 4
N_GRID = 8


def with_ends(drawn, key, low, largest):
    longest = drawn.shape.index(max(drawn.shape))
    spots = []
    for shift in (0, 1):
        where = [jax.random.randint(jax.random.fold_in(key, axis), (), 0, length) for axis, length in enumerate(drawn.shape)]
        where[longest] = (where[longest] + shift) % drawn.shape[longest]
        spots.append(tuple(where))
    return drawn.at[spots[0]].set(low).at[spots[1]].set(largest)


def steps_of(stream_key, dims, split, smallest, top_value):
    gain, own = 1.0, jax.random.fold_in(stream_key, 6)
    for position, shards_of in split:
        steps = jnp.exp(jax.random.uniform(jax.random.fold_in(own, position), (shards_of,), jnp.float32, smallest / len(split), top_value / len(split)))
        gain = gain * jnp.repeat(steps, dims[position] // shards_of).reshape([-1 if axis == position else 1 for axis in range(len(dims))])
    return gain


def centred(stream_key, shape, spread, bound, split=(), dtype=jnp.bfloat16):
    gain = steps_of(stream_key, shape, split, -0.22, 0.18) if split else 1.0
    array = jax.random.normal(stream_key, shape, jnp.float32) * spread * gain
    return jnp.minimum(jnp.maximum(array, -bound), bound).astype(dtype)


def setup_inputs(seed: int = 0) -> dict:
    key_list = jax.random.split(jax.random.key(seed), 7)
    return {
        "l_panels": centred(key_list[0], (N_LAYER, PANELS, S, W), 1.0, 6.0, ((0, 4), (2, 8))),
        "u_panels": centred(key_list[1], (N_LAYER, PANELS, W, C), (16 * PANELS * W) ** -0.5, 0.046875, ((0, 4), (2, 8))),
        "panel_fill": with_ends((jax.random.randint(key_list[2], (N_LAYER, PANELS, S // BLOCK, W // BLOCK), 0, 4) < 3).astype(jnp.int32), jax.random.fold_in(key_list[2], 1), 0, 1),
        "copy_fill": with_ends((jax.random.randint(key_list[3], (N_LAYER, S // BLOCK, C // BLOCK), 0, 4) < 3).astype(jnp.int32), jax.random.fold_in(key_list[3], 1), 0, 1),
        "sep_panels": centred(key_list[4], (NODES, S, WS), (2 * WS) ** -0.5, 0.25, ((1, 8),)),
        "sep_owner": jax.random.randint(key_list[5], (NODES,), 0, N_GRID).astype(jnp.int32),
    }


def reference(l_panels, u_panels, panel_fill, copy_fill, sep_panels, sep_owner):
    row_count = S // N_GRID

    def layer_copy(layer_id):
        fill_panel = panel_fill[layer_id].astype(jnp.bfloat16)
        masked = (l_panels[layer_id].reshape(PANELS, S // BLOCK, BLOCK, W // BLOCK, BLOCK) * fill_panel[:, :, None, :, None]).reshape(PANELS, S, W)
        left_panel = jnp.concatenate([masked[k] for k in range(PANELS)], axis=1)
        right_panel = u_panels[layer_id].reshape(PANELS * W, C)
        update = jnp.dot(left_panel, right_panel, preferred_element_type=jnp.float32)
        fill_copy = copy_fill[layer_id].astype(jnp.float32)
        return -(update.reshape(S // BLOCK, BLOCK, C // BLOCK, BLOCK) * fill_copy[:, None, :, None]).reshape(S, C)

    def combine(low_layer, group_size):
        if group_size == 1:
            return layer_copy(low_layer)
        half_size = group_size // 2
        combined = combine(low_layer, half_size) + combine(low_layer + half_size, half_size)
        level_index = half_size.bit_length() - 1
        node_index = N_LAYER - (N_LAYER >> level_index) + low_layer // group_size
        owner_index = sep_owner[node_index].astype(jnp.int32)
        pivot_rows = lax.dynamic_slice_in_dim(combined, owner_index * row_count, WS, 0).astype(jnp.bfloat16)
        return combined - jnp.dot(sep_panels[node_index], pivot_rows, preferred_element_type=jnp.float32)

    return combine(0, N_LAYER)
```

```python
import jax
import jax.numpy as jnp
from jax import lax
from jax.experimental import pallas as pl
from jax.experimental.pallas import tpu as pltpu
from jax.sharding import PartitionSpec as P

BLOCK = 128
WS = 256
BOTH = ("layer", "grid")
VMEM = pl.BlockSpec(memory_space=pltpu.VMEM)
SMEM = pl.BlockSpec(memory_space=pltpu.SMEM)


def kernel_call(body, out_shape, in_specs, scratch=(), flops=0, nbytes=0):
    many = isinstance(out_shape, (tuple, list))
    return pl.pallas_call(
        body,
        out_shape=out_shape,
        in_specs=in_specs,
        out_specs=[VMEM] * len(out_shape) if many else VMEM,
        scratch_shapes=list(scratch),
        compiler_params=pltpu.CompilerParams(vmem_limit_bytes=40 << 20),
        cost_estimate=pl.CostEstimate(flops=flops, bytes_accessed=nbytes, transcendentals=0),
    )


def apart(x, axis, distance):
    return lax.ppermute(x, axis, [(i, i ^ distance) for i in range(lax.axis_size(axis))])


def gather_grid(x):
    count = lax.axis_size("grid")
    found = [x] + [None] * (count - 1)
    for k in range(2, count, 2):
        found[k] = apart(x, "grid", k)
    for k in range(0, count, 2):
        found[k + 1] = apart(found[k], "grid", 1)
    return found


def mask_panels(l_panels, panel_fill):
    _, panels, rows, width = l_panels.shape

    def body(l_ref, fill_ref, out_ref):
        for k in range(panels):
            for b in range(rows // BLOCK):
                for j in range(width // BLOCK):
                    r = slice(b * BLOCK, (b + 1) * BLOCK)
                    here = fill_ref[0, k, b, j] != 0
                    tile = l_ref[0, k, r, j * BLOCK : (j + 1) * BLOCK]
                    at = k * width + j * BLOCK
                    out_ref[r, at : at + BLOCK] = jnp.where(here, tile, jnp.zeros_like(tile))

    return kernel_call(
        body,
        jax.ShapeDtypeStruct((rows, panels * width), jnp.bfloat16),
        [VMEM, SMEM],
        nbytes=4 * panels * rows * width,
    )(l_panels, panel_fill)


def layer_copy(masked, pieces, copy_fill, place):
    rows, depth = masked.shape
    _, panels, share, columns = pieces[0].shape
    layers, grids = lax.axis_size("layer"), lax.axis_size("grid")
    width = columns // layers
    piece_rows = WS // grids
    step = min(rows, 256)

    def body(*refs):
        place_ref, fill_ref, l_ref = refs[:3]
        u_refs = refs[3 : 3 + grids]
        keep_ref, send_ref, pivot_ref, u_all = refs[3 + grids :]
        core, me = place_ref[0], place_ref[1]
        for k in range(grids):
            for p in range(panels):
                at = pl.multiple_of((p * grids + (me ^ k)) * share, share)
                u_all[pl.ds(at, share), :] = u_refs[k][0, p]
        for r in range(0, rows, step):
            part = jnp.dot(l_ref[r : r + step, :], u_all[...], preferred_element_type=jnp.float32)
            for b in range(0, step, BLOCK):
                here = slice(r + b, r + b + BLOCK)
                for j in range(layers):
                    tiles = []
                    for c in range(j * width, (j + 1) * width, BLOCK):
                        fill = fill_ref[0, (r + b) // BLOCK, c // BLOCK].astype(jnp.float32)
                        tiles.append(part[b : b + BLOCK, c : c + BLOCK] * -fill)
                    tile = tiles[0] if len(tiles) == 1 else jnp.concatenate(tiles, 1)

                    @pl.when(core == j % 2)
                    def _():
                        keep_ref[j // 2, here, :] = tile

                    @pl.when(core != j % 2)
                    def _():
                        send_ref[j // 2, here, :] = tile.astype(jnp.bfloat16)

                    if r + b < WS:
                        low = tile.astype(jnp.bfloat16)
                        for g in range(BLOCK // piece_rows):
                            at = (r + b) // piece_rows + g
                            pivot_ref[j, at] = low[g * piece_rows : (g + 1) * piece_rows]

    return kernel_call(
        body,
        (
            jax.ShapeDtypeStruct((layers // 2, rows, width), jnp.float32),
            jax.ShapeDtypeStruct((layers // 2, rows, width), jnp.bfloat16),
            jax.ShapeDtypeStruct((layers, grids, piece_rows, width), jnp.bfloat16),
        ),
        [SMEM, SMEM, VMEM] + [VMEM] * grids,
        scratch=[pltpu.VMEM((depth, columns), jnp.bfloat16)],
        flops=2 * rows * depth * columns,
        nbytes=2 * rows * depth + 2 * depth * columns + 6 * rows * columns,
    )(place, copy_fill, masked, *pieces)


def tree(layers):
    nodes, level = [], 0
    while 2 << level <= layers:
        size = 2 << level
        for j in range(layers // size):
            low = j * size
            below = [n for n, first, span, _ in nodes if low <= first < low + size]
            nodes.append((layers - (layers >> level) + j, low, size, below))
        level += 1
    return nodes


def pick_pivots(candidates, sep_owner, grids):
    layers, _, piece_rows, width = candidates.shape
    nodes = tree(layers)

    def body(owner_ref, c_ref, out_ref):
        for node, low, size, _ in nodes:
            owner = owner_ref[node]
            total = c_ref[low, owner].astype(jnp.float32)
            for i in range(low + 1, low + size):
                total = total + c_ref[i, owner].astype(jnp.float32)
            total = total.astype(jnp.bfloat16)
            for g in range(grids):
                out_ref[g, node] = total

    return kernel_call(
        body,
        jax.ShapeDtypeStruct((grids, len(nodes), piece_rows, width), jnp.bfloat16),
        [SMEM, VMEM],
        nbytes=4 * candidates.size,
    )(sep_owner, candidates)


def eliminate(own, other, pivots, below_rows, sep_panels):
    rows, width = own.shape
    grids, count, piece_rows, _ = pivots.shape
    nodes = tree(count + 1)
    inner = [n for n in nodes if n[3]]
    step = min(rows, 256)

    def body(own_ref, other_ref, p_ref, below_ref, sep_ref, out_ref, all_p):
        for node, _, _, below in nodes:
            at = node * WS
            for g in range(grids):
                all_p[at + g * piece_rows : at + (g + 1) * piece_rows, :] = p_ref[g, node]
            if below:
                which = [n[0] for n in inner].index(node)
                pivot = all_p[at : at + WS, :].astype(jnp.float32)
                for m in below:
                    pivot = pivot - jnp.dot(
                        below_ref[which, m], all_p[m * WS : (m + 1) * WS, :], preferred_element_type=jnp.float32
                    )
                all_p[at : at + WS, :] = pivot.astype(jnp.bfloat16)
        for r in range(0, rows, step):
            here = slice(r, r + step)
            total = own_ref[here, :] + other_ref[here, :].astype(jnp.float32)
            for node in range(count):
                total = total - jnp.dot(
                    sep_ref[node, here, :], all_p[node * WS : (node + 1) * WS, :], preferred_element_type=jnp.float32
                )
            out_ref[here, :] = total

    return kernel_call(
        body,
        jax.ShapeDtypeStruct((rows, width), jnp.float32),
        [VMEM] * 5,
        scratch=[pltpu.VMEM((count * WS, width), jnp.bfloat16)],
        flops=2 * rows * count * WS * width,
        nbytes=10 * rows * width + 2 * sep_panels.size,
    )(own, other, pivots, below_rows, sep_panels)


def rows_below(sep_panels, sep_owner):
    layers, grids = lax.axis_size("layer"), lax.axis_size("grid")
    inner = [n for n in tree(layers) if n[3]]
    wide = max(max(n[3]) for n in inner) + 1
    shares = layers if WS % (layers * grids * 8) == 0 else 1
    part = WS // shares
    mine = sep_panels[:wide, :WS]
    if shares > 1:
        mine = lax.dynamic_slice_in_dim(mine, lax.axis_index("layer") * part, part, 1)
    piece = part // grids
    mine = mine.reshape(wide, grids, piece, WS).swapaxes(0, 1)
    got = lax.all_to_all(mine, "grid", 0, 0)
    picked = jnp.stack([lax.dynamic_index_in_dim(got, sep_owner[n[0]], 0, keepdims=False) for n in inner])
    axis = BOTH if shares > 1 else "grid"
    spread = jnp.broadcast_to(picked[None], (shares * grids,) + picked.shape)
    full = lax.all_to_all(spread, axis, 0, 0)
    full = jnp.moveaxis(full, 0, 2)
    return full.reshape(len(inner), wide, WS, WS)


def local(l_panels, u_panels, panel_fill, copy_fill, sep_panels, sep_owner):
    layers, grids = lax.axis_size("layer"), lax.axis_size("grid")
    layer, me = lax.axis_index("layer"), lax.axis_index("grid")
    place = jnp.stack([layer % 2, me]).astype(jnp.int32)

    pieces = gather_grid(u_panels)
    masked = mask_panels(l_panels, panel_fill)
    below = rows_below(sep_panels, sep_owner)

    keep, send, candidates = layer_copy(masked, pieces, copy_fill, place)
    shape = candidates.shape
    candidates = lax.all_to_all(candidates.reshape((layers * grids,) + shape[2:]), BOTH, 0, 0).reshape(shape)
    pivots = lax.all_to_all(pick_pivots(candidates, sep_owner, grids), "grid", 0, 0)

    other = apart(send, "layer", 1)
    bit = 1
    while keep.shape[0] > 1:
        bit *= 2
        half = keep.shape[0] // 2
        total = keep + other.astype(jnp.float32)
        total = total.reshape((half, 2) + total.shape[1:])
        side = (layer // bit) % 2
        keep = lax.dynamic_index_in_dim(total, side, 1, keepdims=False)
        send = lax.dynamic_index_in_dim(total, 1 - side, 1, keepdims=False).astype(jnp.bfloat16)
        other = apart(send, "layer", bit)
    return eliminate(keep[0], other[0], pivots, below, sep_panels)


def solution(mesh):
    return jax.shard_map(
        local,
        mesh=mesh,
        in_specs=(
            P("layer", None, "grid", None),
            P("layer", None, "grid", None),
            P("layer", None, "grid", None),
            P("layer", "grid", None),
            P(None, "grid", None),
            P(),
        ),
        out_specs=P("grid", "layer"),
        check_vma=False,
    )
```

```python
import jax
import jax.numpy as jnp
from jax import lax
from jax.experimental import pallas as pl
from jax.experimental.pallas import tpu as pltpu
from jax.sharding import PartitionSpec as P

BLOCK = 128
WS = 256
VMEM_LIMIT = 40 << 20
EARLY_LIMIT = 60 << 20
BOTH = ("layer", "grid")
VMEM = pl.BlockSpec(memory_space=pltpu.VMEM)
HBM = pl.BlockSpec(memory_space=pltpu.HBM)
ANY = pl.BlockSpec(memory_space=pl.ANY)
SMEM = pl.BlockSpec(memory_space=pltpu.SMEM)


def kernel_call(body, out_shape, in_specs, scratch=(), flops=0, nbytes=0, limit=VMEM_LIMIT):
    many = isinstance(out_shape, (tuple, list))
    return pl.pallas_call(
        body,
        out_shape=out_shape,
        in_specs=in_specs,
        out_specs=[VMEM] * len(out_shape) if many else VMEM,
        scratch_shapes=list(scratch),
        compiler_params=pltpu.CompilerParams(vmem_limit_bytes=limit),
        cost_estimate=pl.CostEstimate(flops=flops, bytes_accessed=nbytes, transcendentals=0),
    )


def apart(x, axis, distance):
    return lax.ppermute(x, axis, [(i, i ^ distance) for i in range(lax.axis_size(axis))])


def bits(count):
    return [1 << i for i in range(count.bit_length() - 1)]


def gather_grid(x):
    count = lax.axis_size("grid")
    found = [x] + [None] * (count - 1)
    for k in range(2, count, 2):
        found[k] = apart(x, "grid", k)
    for k in range(0, count, 2):
        found[k + 1] = apart(found[k], "grid", 1)
    return found


def pick_below(sep_panels, sep_owner, place, after):
    layers = lax.axis_size("layer")
    inner = [n for n in tree(layers) if n[3]]
    wide = max(max(n[3]) for n in inner) + 1
    part = WS // layers

    def body(place_ref, owner_ref, sep_ref, _, out_ref, held, sem):
        start = pl.multiple_of(place_ref[0] * part, part)
        copy = pltpu.make_async_copy(sep_ref.at[:wide, pl.ds(start, part)], held, sem)
        copy.start()
        copy.wait()
        for i, n in enumerate(inner):
            mine = owner_ref[n[0]] == place_ref[1]
            out_ref[i] = jnp.where(mine, held[...], jnp.zeros(held.shape, held.dtype))

    return kernel_call(
        body,
        jax.ShapeDtypeStruct((len(inner), wide, part, WS), jnp.bfloat16),
        [SMEM, SMEM, HBM, ANY],
        scratch=[pltpu.VMEM((wide, part, WS), jnp.bfloat16), pltpu.SemaphoreType.DMA],
        nbytes=4 * wide * part * WS,
        limit=EARLY_LIMIT,
    )(place, sep_owner, sep_panels, after)


def mask_panels(l_panels, panel_fill, place, after):
    _, panels, rows, width = l_panels.shape
    share = width // lax.axis_size("grid")
    step = min(rows, 256)

    def body(place_ref, fill_ref, l_ref, _, out_ref, l_all, sems):
        first = place_ref[1] * share // BLOCK
        copies = [
            pltpu.make_async_copy(l_ref.at[0, :, r : r + step], l_all.at[:, r : r + step], sems.at[r // step])
            for r in range(0, rows, step)
        ]
        for copy in copies:
            copy.start()
        for r in range(0, rows, step):
            copies[r // step].wait()
            for k in range(panels):
                for j in range(width // BLOCK):
                    at = pl.multiple_of(((j ^ first) * panels + k) * BLOCK, BLOCK)
                    for b in range(r, r + step, BLOCK):
                        here = fill_ref[0, k, j, b // BLOCK] != 0
                        tile = l_all[k, b : b + BLOCK, j * BLOCK : (j + 1) * BLOCK]
                        out_ref[b : b + BLOCK, pl.ds(at, BLOCK)] = jnp.where(here, tile, jnp.zeros_like(tile))

    return kernel_call(
        body,
        jax.ShapeDtypeStruct((rows, panels * width), jnp.bfloat16),
        [SMEM, SMEM, HBM, ANY],
        scratch=[pltpu.VMEM((panels, rows, width), jnp.bfloat16), pltpu.SemaphoreType.DMA((rows // step,))],
        nbytes=4 * panels * rows * width,
    )(place, panel_fill, l_panels, after)


def load_panels(u_refs, first, grids, u_all, sems, me):
    _, panels, share, _ = u_refs[0].shape
    copies = []
    for i, ref in enumerate(u_refs):
        block, inside = i * share // BLOCK, (me ^ (first + i)) * share % BLOCK
        for p in range(panels):
            at = pl.multiple_of((block * panels + p) * BLOCK + inside, share)
            copies.append(pltpu.make_async_copy(ref.at[0, p], u_all.at[pl.ds(at, share), :], sems.at[i, p]))
            copies[-1].start()
    return copies


def block_fill(part, fill_ref, row, low, high):
    lines = []
    for b in range(0, part.shape[0], BLOCK):
        tiles = []
        for c in range(low, high, BLOCK):
            fill = fill_ref[0, c // BLOCK, (row + b) // BLOCK].astype(jnp.float32)
            tiles.append(part[b : b + BLOCK, c : c + BLOCK] * -fill)
        lines.append(tiles[0] if len(tiles) == 1 else jnp.concatenate(tiles, 1))
    return lines[0] if len(lines) == 1 else jnp.concatenate(lines, 0)


def first_part(masked, pieces, grids, place, after):
    rows, _ = masked.shape
    _, panels, share, columns = pieces[0].shape
    depth = panels * share * len(pieces)
    step = min(rows, 256)

    def body(place_ref, l_ref, *refs):
        u_refs, (out_ref, u_all, sems) = refs[: len(pieces)], refs[len(pieces) + 1 :]
        for copy in load_panels(u_refs, 0, grids, u_all, sems, place_ref[1]):
            copy.wait()
        for r in range(0, rows, step):
            here = slice(r, r + step)
            out_ref[here, :] = jnp.dot(l_ref[here, :depth], u_all[...], preferred_element_type=jnp.float32)

    return kernel_call(
        body,
        jax.ShapeDtypeStruct((rows, columns), jnp.float32),
        [SMEM, VMEM] + [HBM] * len(pieces) + [ANY],
        scratch=[pltpu.VMEM((depth, columns), jnp.bfloat16), pltpu.SemaphoreType.DMA((len(pieces), panels))],
        flops=2 * rows * depth * columns,
        nbytes=2 * rows * depth + 2 * depth * columns + 4 * rows * columns,
    )(place, masked, *pieces, after)


def layer_copy(begun, masked, pieces, grids, copy_fill, place, after):
    rows, columns = begun.shape
    _, panels, share, _ = pieces[0].shape
    layers = lax.axis_size("layer")
    width = columns // layers
    piece_rows = WS // grids
    step = min(rows, 256)
    depth = panels * share * len(pieces)
    done = masked.shape[1] - depth

    def body(place_ref, fill_ref, begun_ref, l_ref, *refs):
        u_refs, (keep_ref, send_ref, pivot_ref, u_all, sems) = refs[: len(pieces)], refs[len(pieces) + 1 :]
        core = place_ref[0] % 2
        for copy in load_panels(u_refs, grids - len(pieces), grids, u_all, sems, place_ref[1]):
            copy.wait()
        for r in range(0, rows, step):
            here = slice(r, r + step)
            part = begun_ref[here, :] + jnp.dot(l_ref[here, done:], u_all[...], preferred_element_type=jnp.float32)
            for j in range(layers):
                tile = block_fill(part, fill_ref, r, j * width, (j + 1) * width)

                @pl.when(core == j % 2)
                def _():
                    keep_ref[j // 2, here, :] = tile

                @pl.when(core != j % 2)
                def _():
                    send_ref[j // 2, here, :] = tile.astype(jnp.bfloat16)

                if r < WS:
                    low = tile.astype(jnp.bfloat16)
                    for g in range(step // piece_rows):
                        pivot_ref[j, r // piece_rows + g] = low[g * piece_rows : (g + 1) * piece_rows]

    return kernel_call(
        body,
        (
            jax.ShapeDtypeStruct((layers // 2, rows, width), jnp.float32),
            jax.ShapeDtypeStruct((layers // 2, rows, width), jnp.bfloat16),
            jax.ShapeDtypeStruct((layers, grids, piece_rows, width), jnp.bfloat16),
        ),
        [SMEM, SMEM, VMEM, VMEM] + [HBM] * len(pieces) + [ANY],
        scratch=[pltpu.VMEM((depth, columns), jnp.bfloat16), pltpu.SemaphoreType.DMA((len(pieces), panels))],
        flops=2 * rows * depth * columns,
        nbytes=2 * rows * depth + 2 * depth * columns + 8 * rows * columns,
    )(place, copy_fill, begun, masked, *pieces, after)


def tree(layers):
    nodes, level = [], 0
    while 2 << level <= layers:
        size = 2 << level
        for j in range(layers // size):
            low = j * size
            below = [n for n, first, span, _ in nodes if low <= first < low + size]
            nodes.append((layers - (layers >> level) + j, low, size, below))
        level += 1
    return nodes


def pick_pivots(candidates, sep_owner, grids, after):
    layers, _, piece_rows, width = candidates.shape
    nodes = tree(layers)

    def body(owner_ref, c_ref, *refs):
        out_ref = refs[-1]
        for node, low, size, _ in nodes:
            owner = owner_ref[node]
            total = c_ref[low, owner].astype(jnp.float32)
            for i in range(low + 1, low + size):
                total = total + c_ref[i, owner].astype(jnp.float32)
            total = total.astype(jnp.bfloat16)
            for g in range(grids):
                out_ref[g, node] = total

    return kernel_call(
        body,
        jax.ShapeDtypeStruct((grids, len(nodes), piece_rows, width), jnp.bfloat16),
        [SMEM, VMEM] + [ANY] * len(after),
        nbytes=4 * candidates.size,
    )(sep_owner, candidates, *after)


def eliminate(own, other, pivots, below, sep_panels, place):
    rows, width = own.shape
    grids, count, piece_rows, _ = pivots.shape
    nodes = tree(count + 1)
    inner = [n for n in nodes if n[3]]
    _, wide, part, _ = below[0].shape
    step = min(rows, 256)

    def body(place_ref, own_ref, other_ref, p_ref, sep_ref, *refs):
        below_refs = refs[: len(below)]
        out_ref, all_p, all_below = refs[len(below) :]
        layer = place_ref[0]
        for k, ref in enumerate(below_refs):
            at = pl.multiple_of((layer ^ k if len(below) > 1 else 0) * part, part)
            for i in range(len(inner)):
                for m in inner[i][3]:
                    all_below[i, m, pl.ds(at, part), :] = ref[i, m]
        for node, _, _, under in nodes:
            at = node * WS
            for g in range(grids):
                all_p[at + g * piece_rows : at + (g + 1) * piece_rows, :] = p_ref[g, node]
            if under:
                which = [n[0] for n in inner].index(node)
                pivot = all_p[at : at + WS, :].astype(jnp.float32)
                for m in under:
                    pivot = pivot - jnp.dot(
                        all_below[which, m], all_p[m * WS : (m + 1) * WS, :], preferred_element_type=jnp.float32
                    )
                all_p[at : at + WS, :] = pivot.astype(jnp.bfloat16)
        for r in range(0, rows, step):
            here = slice(r, r + step)
            total = own_ref[here, :] + other_ref[here, :].astype(jnp.float32)
            for node in range(count):
                total = total - jnp.dot(
                    sep_ref[node, here, :], all_p[node * WS : (node + 1) * WS, :], preferred_element_type=jnp.float32
                )
            out_ref[here, :] = total

    return kernel_call(
        body,
        jax.ShapeDtypeStruct((rows, width), jnp.float32),
        [SMEM] + [VMEM] * (4 + len(below)),
        scratch=[
            pltpu.VMEM((count * WS, width), jnp.bfloat16),
            pltpu.VMEM((len(inner), wide, WS, WS), jnp.bfloat16),
        ],
        flops=2 * rows * count * WS * width,
        nbytes=10 * rows * width + 2 * sep_panels.size,
    )(place, own, other, pivots, sep_panels, *below)


def parts_below(part):
    found = [part]
    while len(found) < lax.axis_size("layer"):
        found += [apart(x, "layer", len(found)) for x in found]
    return found


def local(l_panels, u_panels, panel_fill, copy_fill, sep_panels, sep_owner):
    layers, grids = lax.axis_size("layer"), lax.axis_size("grid")
    layer, me = lax.axis_index("layer"), lax.axis_index("grid")
    place = jnp.stack([layer, me]).astype(jnp.int32)

    pieces = gather_grid(u_panels)
    below = pick_below(sep_panels, sep_owner, place, pieces[1])
    masked = mask_panels(l_panels, jnp.swapaxes(panel_fill, 2, 3), place, below)
    for bit in bits(grids)[:2]:
        below = below + apart(below, "grid", bit)

    last = grids * BLOCK // l_panels.shape[3]
    begun = first_part(masked, pieces[:-last], grids, place, below)
    for bit in bits(grids)[2:]:
        below = below + apart(below, "grid", bit)
    keep, send, candidates = layer_copy(
        begun, masked, pieces[-last:], grids, jnp.swapaxes(copy_fill, 1, 2), place, below
    )
    below = parts_below(below)
    shape = candidates.shape
    candidates = lax.all_to_all(candidates.reshape((layers * grids,) + shape[2:]), BOTH, 0, 0).reshape(shape)

    other = apart(send, "layer", 1)
    pivots = None
    bit = 1
    while keep.shape[0] > 1:
        bit *= 2
        half = keep.shape[0] // 2
        total = keep + other.astype(jnp.float32)
        total = total.reshape((half, 2) + total.shape[1:])
        side = (layer // bit) % 2
        keep = lax.dynamic_index_in_dim(total, side, 1, keepdims=False)
        send = lax.dynamic_index_in_dim(total, 1 - side, 1, keepdims=False).astype(jnp.bfloat16)
        if pivots is None:
            pivots = lax.all_to_all(pick_pivots(candidates, sep_owner, grids, [send] + below), "grid", 0, 0)
        other = apart(send, "layer", bit)
    return eliminate(keep[0], other[0], pivots, below, sep_panels, place)


def solution(mesh):
    return jax.shard_map(
        local,
        mesh=mesh,
        in_specs=(
            P("layer", None, "grid", None),
            P("layer", None, "grid", None),
            P("layer", None, "grid", None),
            P("layer", "grid", None),
            P(None, "grid", None),
            P(),
        ),
        out_specs=P("grid", "layer"),
        check_vma=False,
    )
```

```python
import jax
import jax.numpy as jnp
from jax import lax
from jax.experimental import pallas as pl
from jax.experimental.pallas import tpu as pltpu
from jax.sharding import PartitionSpec as P

BLOCK = 128
WS = 256
VMEM_LIMIT = 40 << 20
EARLY_LIMIT = 60 << 20
BOTH = ("layer", "grid")
VMEM = pl.BlockSpec(memory_space=pltpu.VMEM)
HBM = pl.BlockSpec(memory_space=pltpu.HBM)
ANY = pl.BlockSpec(memory_space=pl.ANY)
SMEM = pl.BlockSpec(memory_space=pltpu.SMEM)


def kernel_call(body, out_shape, in_specs, scratch=(), flops=0, nbytes=0, limit=VMEM_LIMIT):
    many = isinstance(out_shape, (tuple, list))
    return pl.pallas_call(
        body,
        out_shape=out_shape,
        in_specs=in_specs,
        out_specs=[VMEM] * len(out_shape) if many else VMEM,
        scratch_shapes=list(scratch),
        compiler_params=pltpu.CompilerParams(vmem_limit_bytes=limit),
        cost_estimate=pl.CostEstimate(flops=flops, bytes_accessed=nbytes, transcendentals=0),
    )


def apart(x, axis, distance):
    return lax.ppermute(x, axis, [(i, i ^ distance) for i in range(lax.axis_size(axis))])


def masks(count):
    top = count.bit_length() - 1
    return [3 << i - 1 for i in range(top - 1, 1, -1)] + [1 << i for i in (1, 0) if i < top]


def together(*xs):
    return lax.optimization_barrier(xs)


def pick_below(sep_panels, sep_owner):
    inner = [n for n in tree(lax.axis_size("layer")) if n[3]]
    wide = max(max(n[3]) for n in inner) + 1
    part = WS // lax.axis_size("layer")

    def body(owner_ref, sep_ref, out_ref, held, sem):
        start = pl.multiple_of(lax.axis_index("layer") * part, part)
        copy = pltpu.make_async_copy(sep_ref.at[:wide, pl.ds(start, part)], held, sem)
        copy.start()
        copy.wait()
        for i, n in enumerate(inner):
            mine = owner_ref[n[0]] == lax.axis_index("grid")
            out_ref[i] = jnp.where(mine, held[...], jnp.zeros(held.shape, held.dtype))

    return kernel_call(
        body,
        jax.ShapeDtypeStruct((len(inner), wide, part, WS), jnp.bfloat16),
        [SMEM, HBM],
        scratch=[pltpu.VMEM((wide, part, WS), jnp.bfloat16), pltpu.SemaphoreType.DMA],
        nbytes=4 * wide * part * WS,
        limit=EARLY_LIMIT,
    )(sep_owner, sep_panels)


def mask_panels(l_panels, panel_fill, order):
    _, panels, rows, width = l_panels.shape
    share = width // lax.axis_size("grid")
    step = min(rows, 256)

    def body(fill_ref, l_ref, out_ref, l_all, sems):
        first = lax.axis_index("grid") * share // BLOCK
        copies = [
            pltpu.make_async_copy(l_ref.at[0, :, r : r + step], l_all.at[:, r : r + step], sems.at[r // step])
            for r in range(0, rows, step)
        ]
        for copy in copies:
            copy.start()
        for r in range(0, rows, step):
            copies[r // step].wait()
            for i, block in enumerate(order):
                j = first ^ block
                for k in range(panels):
                    at = (i * panels + k) * BLOCK
                    for b in range(r, r + step, BLOCK):
                        here = fill_ref[0, k, j, b // BLOCK] != 0
                        tile = l_all[k, b : b + BLOCK, pl.ds(pl.multiple_of(j * BLOCK, BLOCK), BLOCK)]
                        out_ref[b : b + BLOCK, at : at + BLOCK] = jnp.where(here, tile, jnp.zeros_like(tile))

    return kernel_call(
        body,
        jax.ShapeDtypeStruct((rows, panels * width), jnp.bfloat16),
        [SMEM, HBM],
        scratch=[pltpu.VMEM((panels, rows, width), jnp.bfloat16), pltpu.SemaphoreType.DMA((rows // step,))],
        nbytes=4 * panels * rows * width,
    )(panel_fill, pltpu.with_memory_space_constraint(l_panels, pltpu.HBM))


def load_panels(u_refs, pieces, order, u_all, sems, me):
    _, panels, share, _ = u_refs[0].shape
    copies = []
    for i, (k, ref) in enumerate(zip(pieces, u_refs)):
        block, inside = order.index(k * share // BLOCK), (me ^ k) * share % BLOCK
        for p in range(panels):
            at = pl.multiple_of((block * panels + p) * BLOCK + inside, share)
            copies.append(pltpu.make_async_copy(ref.at[0, p], u_all.at[pl.ds(at, share), :], sems.at[i, p]))
            copies[-1].start()
    return copies


def first_part(masked, pieces, order):
    rows, _ = masked.shape
    _, panels, share, columns = pieces[0].shape
    depth = panels * share * len(pieces)
    step = min(rows, 256)

    def body(l_ref, *refs):
        u_refs, (out_ref, u_all, sems) = refs[: len(pieces)], refs[len(pieces) :]
        for copy in load_panels(u_refs, list(pieces), order, u_all, sems, lax.axis_index("grid")):
            copy.wait()
        for r in range(0, rows, step):
            here = slice(r, r + step)
            out_ref[here, :] = jnp.dot(l_ref[here, :depth], u_all[...], preferred_element_type=jnp.float32)

    return kernel_call(
        body,
        jax.ShapeDtypeStruct((rows, columns), jnp.float32),
        [VMEM] + [HBM] * len(pieces),
        scratch=[pltpu.VMEM((depth, columns), jnp.bfloat16), pltpu.SemaphoreType.DMA((len(pieces), panels))],
        flops=2 * rows * depth * columns,
        nbytes=2 * rows * depth + 2 * depth * columns + 4 * rows * columns,
    )(masked, *pieces.values())


def layer_copy(begun, masked, pieces, order, grids, copy_fill):
    rows, columns = begun.shape
    panels, share = next(iter(pieces.values())).shape[1:3]
    layers = lax.axis_size("layer")
    width = columns // layers
    piece_rows = WS // grids
    step = min(rows, 256)
    depth = panels * share * len(pieces)
    done = masked.shape[1] - depth

    def body(fill_ref, begun_ref, l_ref, *refs):
        u_refs, (keep_ref, send_ref, pivot_ref, u_all, sums, sems) = refs[: len(pieces)], refs[len(pieces) :]
        core = lax.rem(lax.axis_index("layer"), 2)
        for copy in load_panels(u_refs, list(pieces), order[-(depth // panels // BLOCK) :], u_all, sems, lax.axis_index("grid")):
            copy.wait()

        def filled(slot, j, row, count):
            start = pl.multiple_of(j * width, width)
            lines = []
            for b in range(row, row + count, BLOCK):
                tiles = []
                for c in range(0, width, BLOCK):
                    fill = fill_ref[0, j * (width // BLOCK) + c // BLOCK, b // BLOCK].astype(jnp.float32)
                    tiles.append(sums[slot, b - row : b - row + BLOCK, pl.ds(start + c, BLOCK)] * -fill)
                lines.append(tiles[0] if len(tiles) == 1 else jnp.concatenate(tiles, 1))
            return lines[0] if len(lines) == 1 else jnp.concatenate(lines, 0)

        for r in range(0, rows, step):
            here, slot = slice(r, r + step), r // step % 2
            sums[slot] = begun_ref[here, :] + jnp.dot(
                l_ref[here, done:], u_all[...], preferred_element_type=jnp.float32
            )
            if r < WS:
                for j in range(layers):
                    low = filled(slot, j, r, step).astype(jnp.bfloat16)
                    for g in range(step // piece_rows):
                        pivot_ref[j, r // piece_rows + g] = low[g * piece_rows : (g + 1) * piece_rows]
            for i in range(layers // 2):
                keep_ref[i, here, :] = filled(slot, 2 * i + core, r, step)
                send_ref[i, here, :] = filled(slot, 2 * i + 1 - core, r, step).astype(jnp.bfloat16)

    return kernel_call(
        body,
        (
            jax.ShapeDtypeStruct((layers // 2, rows, width), jnp.float32),
            jax.ShapeDtypeStruct((layers // 2, rows, width), jnp.bfloat16),
            jax.ShapeDtypeStruct((layers, grids, piece_rows, width), jnp.bfloat16),
        ),
        [SMEM, VMEM, VMEM] + [HBM] * len(pieces),
        scratch=[
            pltpu.VMEM((depth, columns), jnp.bfloat16),
            pltpu.VMEM((2, step, columns), jnp.float32),
            pltpu.SemaphoreType.DMA((len(pieces), panels)),
        ],
        flops=2 * rows * depth * columns,
        nbytes=2 * rows * depth + 2 * depth * columns + 8 * rows * columns,
    )(copy_fill, begun, masked, *pieces.values())


def tree(layers):
    nodes, level = [], 0
    while 2 << level <= layers:
        size = 2 << level
        for j in range(layers // size):
            low = j * size
            below = [n for n, first, span, _ in nodes if low <= first < low + size]
            nodes.append((layers - (layers >> level) + j, low, size, below))
        level += 1
    return nodes


def pick_pivots(candidates, sep_owner, grids, after):
    layers, _, piece_rows, width = candidates.shape
    nodes = tree(layers)

    def body(owner_ref, c_ref, *refs):
        out_ref = refs[-1]
        for node, low, size, _ in nodes:
            owner = owner_ref[node]
            total = c_ref[low, owner].astype(jnp.float32)
            for i in range(low + 1, low + size):
                total = total + c_ref[i, owner].astype(jnp.float32)
            total = total.astype(jnp.bfloat16)
            for g in range(grids):
                out_ref[g, node] = total

    return kernel_call(
        body,
        jax.ShapeDtypeStruct((grids, len(nodes), piece_rows, width), jnp.bfloat16),
        [SMEM, VMEM] + [ANY] * len(after),
        nbytes=4 * candidates.size,
    )(sep_owner, candidates, *after)


def eliminate(own, other, pivots, below, sep_panels):
    rows, width = own.shape
    grids, count, piece_rows, _ = pivots.shape
    nodes = tree(count + 1)
    inner = [n for n in nodes if n[3]]
    _, wide, part, _ = below[0].shape
    step = min(rows, 256)

    def body(own_ref, other_ref, p_ref, sep_ref, *refs):
        below_refs = refs[: len(below)]
        out_ref, all_p, all_below = refs[len(below) :]
        layer = lax.axis_index("layer")
        for k, ref in enumerate(below_refs):
            at = pl.multiple_of((layer ^ k) * part, part)
            for i in range(len(inner)):
                for m in inner[i][3]:
                    all_below[i, m, pl.ds(at, part), :] = ref[i, m]
        for node, _, _, under in nodes:
            at = node * WS
            for g in range(grids):
                all_p[at + g * piece_rows : at + (g + 1) * piece_rows, :] = p_ref[g, node]
            if under:
                which = [n[0] for n in inner].index(node)
                pivot = all_p[at : at + WS, :].astype(jnp.float32)
                for m in under:
                    pivot = pivot - jnp.dot(
                        all_below[which, m], all_p[m * WS : (m + 1) * WS, :], preferred_element_type=jnp.float32
                    )
                all_p[at : at + WS, :] = pivot.astype(jnp.bfloat16)
        for r in range(0, rows, step):
            here = slice(r, r + step)
            total = own_ref[here, :] + other_ref[here, :].astype(jnp.float32)
            for node in range(count):
                total = total - jnp.dot(
                    sep_ref[node, here, :], all_p[node * WS : (node + 1) * WS, :], preferred_element_type=jnp.float32
                )
            out_ref[here, :] = total

    return kernel_call(
        body,
        jax.ShapeDtypeStruct((rows, width), jnp.float32),
        [VMEM] * (4 + len(below)),
        scratch=[
            pltpu.VMEM((count * WS, width), jnp.bfloat16),
            pltpu.VMEM((len(inner), wide, WS, WS), jnp.bfloat16),
        ],
        flops=2 * rows * count * WS * width,
        nbytes=10 * rows * width + 2 * sep_panels.size,
    )(own, other, pivots, sep_panels, *below)


def local(l_panels, u_panels, panel_fill, copy_fill, sep_panels, sep_owner):
    layers, grids = lax.axis_size("layer"), lax.axis_size("grid")
    layer, me = lax.axis_index("layer"), lax.axis_index("grid")

    hops = masks(grids)
    far, near = hops[0], hops[-1]
    pieces = {0: u_panels}
    below = pick_below(sep_panels, sep_owner)
    beside = apart(u_panels, "grid", near)
    for hop in hops[:-1]:
        for k, piece in list(pieces.items()):
            if k == far:
                piece, below = together(piece, below)
            pieces[k ^ hop] = apart(piece, "grid", hop)
    blocks = [k * u_panels.shape[2] // BLOCK for k in pieces]
    order = list(dict.fromkeys(blocks))
    masked = mask_panels(l_panels, jnp.swapaxes(panel_fill, 2, 3), order)
    beside, below = together(beside, below)
    below = below + apart(below, "grid", far)
    last = list(pieces)[-1]
    pieces[near] = beside
    for k in list(pieces)[1:-1]:
        if k == far:
            pieces[k], masked = together(pieces[k], masked)
        if k == last:
            pieces[k], below = together(pieces[k], below)
        pieces[k ^ near] = apart(pieces[k], "grid", near)
    for hop in hops[1:-1]:
        below = below + apart(below, "grid", hop)
    last ^= near
    pieces[last], below = together(pieces[last], below)

    half = len(order) // 2
    early = {k: piece for k, piece in pieces.items() if k * piece.shape[2] // BLOCK in order[:half]}
    late = {k: piece for k, piece in pieces.items() if k not in early}
    begun = first_part(masked, early, order)
    keep, send, candidates = layer_copy(begun, masked, late, order, grids, jnp.swapaxes(copy_fill, 1, 2))
    shape = candidates.shape
    candidates = lax.all_to_all(candidates.reshape((layers * grids,) + shape[2:]), BOTH, 0, 0).reshape(shape)

    below = [below + apart(below, "grid", hops[-1])]
    while len(below) < layers:
        below += [apart(part, "layer", len(below)) for part in below]
    other = apart(send, "layer", 1)
    pivots = None
    bit = 1
    while keep.shape[0] > 1:
        bit *= 2
        half = keep.shape[0] // 2
        total = keep + other.astype(jnp.float32)
        total = total.reshape((half, 2) + total.shape[1:])
        side = (layer // bit) % 2
        keep = lax.dynamic_index_in_dim(total, side, 1, keepdims=False)
        send = lax.dynamic_index_in_dim(total, 1 - side, 1, keepdims=False).astype(jnp.bfloat16)
        if pivots is None:
            pivots = lax.all_to_all(pick_pivots(candidates, sep_owner, grids, [send] + below), "grid", 0, 0)
        other = apart(send, "layer", bit)
    return eliminate(keep[0], other[0], pivots, below, sep_panels)


def solution(mesh):
    return jax.shard_map(
        local,
        mesh=mesh,
        in_specs=(
            P("layer", None, "grid", None),
            P("layer", None, "grid", None),
            P("layer", None, "grid", None),
            P("layer", "grid", None),
            P(None, "grid", None),
            P(),
        ),
        out_specs=P("grid", "layer"),
        check_vma=False,
    )
```

```python
import jax
import jax.numpy as jnp
from jax import lax
from jax.experimental import pallas as pl
from jax.experimental.pallas import tpu as pltpu
from jax.sharding import PartitionSpec as P

BLOCK = 128
WS = 256
VMEM_LIMIT = 40 << 20
EARLY_LIMIT = 60 << 20
BOTH = ("layer", "grid")
VMEM = pl.BlockSpec(memory_space=pltpu.VMEM)
HBM = pl.BlockSpec(memory_space=pltpu.HBM)
ANY = pl.BlockSpec(memory_space=pl.ANY)
SMEM = pl.BlockSpec(memory_space=pltpu.SMEM)


def kernel_call(body, out_shape, in_specs, scratch=(), flops=0, nbytes=0, limit=VMEM_LIMIT):
    many = isinstance(out_shape, (tuple, list))
    return pl.pallas_call(
        body,
        out_shape=out_shape,
        in_specs=in_specs,
        out_specs=[VMEM] * len(out_shape) if many else VMEM,
        scratch_shapes=list(scratch),
        compiler_params=pltpu.CompilerParams(vmem_limit_bytes=limit),
        cost_estimate=pl.CostEstimate(flops=flops, bytes_accessed=nbytes, transcendentals=0),
    )


def apart(x, axis, distance):
    return lax.ppermute(x, axis, [(i, i ^ distance) for i in range(lax.axis_size(axis))])


def masks(count):
    top = count.bit_length() - 1
    return [3 << i - 1 for i in range(top - 1, 1, -1)] + [1 << i for i in (1, 0) if i < top]


def together(*xs):
    return lax.optimization_barrier(xs)


def pick_below(sep_panels, sep_owner):
    inner = [n for n in tree(lax.axis_size("layer")) if n[3]]
    wide = max(max(n[3]) for n in inner) + 1
    part = WS // 2

    def body(owner_ref, sep_ref, out_ref, held, owner, sems):
        start = pl.multiple_of(lax.rem(lax.axis_index("layer"), 2) * part, part)
        copies = [
            pltpu.make_async_copy(owner_ref, owner, sems.at[0]),
            pltpu.make_async_copy(sep_ref.at[:wide, pl.ds(start, part)], held, sems.at[1]),
        ]
        for copy in copies:
            copy.start()
        for copy in copies:
            copy.wait()
        for i, n in enumerate(inner):
            mine = owner[n[0]] == lax.axis_index("grid")
            out_ref[i] = jnp.where(mine, held[...], jnp.zeros(held.shape, held.dtype))

    return kernel_call(
        body,
        jax.ShapeDtypeStruct((len(inner), wide, part, WS), jnp.bfloat16),
        [HBM, HBM],
        scratch=[
            pltpu.VMEM((wide, part, WS), jnp.bfloat16),
            pltpu.SMEM(sep_owner.shape, jnp.int32),
            pltpu.SemaphoreType.DMA((2,)),
        ],
        nbytes=4 * wide * part * WS,
        limit=EARLY_LIMIT,
    )(sep_owner, sep_panels)


def mask_panels(l_panels, panel_fill, order):
    _, panels, rows, width = l_panels.shape
    share = width // lax.axis_size("grid")
    step = min(rows, 256)

    def body(fill_ref, l_ref, out_ref, l_all, sems):
        first = lax.axis_index("grid") * share // BLOCK
        copies = [
            pltpu.make_async_copy(l_ref.at[0, :, r : r + step], l_all.at[:, r : r + step], sems.at[r // step])
            for r in range(0, rows, step)
        ]
        for copy in copies:
            copy.start()
        for r in range(0, rows, step):
            copies[r // step].wait()
            for i, block in enumerate(order):
                j = first ^ block
                for k in range(panels):
                    at = (i * panels + k) * BLOCK
                    for b in range(r, r + step, BLOCK):
                        here = fill_ref[0, k, j, b // BLOCK] != 0
                        tile = l_all[k, b : b + BLOCK, pl.ds(pl.multiple_of(j * BLOCK, BLOCK), BLOCK)]
                        out_ref[b : b + BLOCK, at : at + BLOCK] = jnp.where(here, tile, jnp.zeros_like(tile))

    return kernel_call(
        body,
        jax.ShapeDtypeStruct((rows, panels * width), jnp.bfloat16),
        [SMEM, HBM],
        scratch=[pltpu.VMEM((panels, rows, width), jnp.bfloat16), pltpu.SemaphoreType.DMA((rows // step,))],
        nbytes=4 * panels * rows * width,
    )(panel_fill, pltpu.with_memory_space_constraint(l_panels, pltpu.HBM))


def load_panels(u_refs, pieces, order, u_all, sems, me):
    _, panels, share, _ = u_refs[0].shape
    copies = []
    for i, (k, ref) in enumerate(zip(pieces, u_refs)):
        block, inside = order.index(k * share // BLOCK), (me ^ k) * share % BLOCK
        for p in range(panels):
            at = pl.multiple_of((block * panels + p) * BLOCK + inside, share)
            copies.append(pltpu.make_async_copy(ref.at[0, p], u_all.at[pl.ds(at, share), :], sems.at[i, p]))
            copies[-1].start()
    return copies


def first_part(masked, pieces, order):
    rows, _ = masked.shape
    _, panels, share, columns = pieces[0].shape
    depth = panels * share * len(pieces)
    step = min(rows, 256)

    def body(l_ref, *refs):
        u_refs, (out_ref, u_all, sems) = refs[: len(pieces)], refs[len(pieces) :]
        for copy in load_panels(u_refs, list(pieces), order, u_all, sems, lax.axis_index("grid")):
            copy.wait()
        for r in range(0, rows, step):
            here = slice(r, r + step)
            out_ref[here, :] = jnp.dot(l_ref[here, :depth], u_all[...], preferred_element_type=jnp.float32)

    return kernel_call(
        body,
        jax.ShapeDtypeStruct((rows, columns), jnp.float32),
        [VMEM] + [HBM] * len(pieces),
        scratch=[pltpu.VMEM((depth, columns), jnp.bfloat16), pltpu.SemaphoreType.DMA((len(pieces), panels))],
        flops=2 * rows * depth * columns,
        nbytes=2 * rows * depth + 2 * depth * columns + 4 * rows * columns,
    )(masked, *pieces.values())


def layer_copy(begun, masked, pieces, order, grids, copy_fill):
    rows, columns = begun.shape
    panels, share = next(iter(pieces.values())).shape[1:3]
    layers = lax.axis_size("layer")
    width = columns // layers
    piece_rows = WS // grids
    step = min(rows, 256)
    depth = panels * share * len(pieces)
    done = masked.shape[1] - depth

    def body(fill_ref, begun_ref, l_ref, *refs):
        u_refs, (keep_ref, send_ref, pivot_ref, u_all, sums, sems) = refs[: len(pieces)], refs[len(pieces) :]
        core = lax.rem(lax.axis_index("layer"), 2)
        for copy in load_panels(u_refs, list(pieces), order[-(depth // panels // BLOCK) :], u_all, sems, lax.axis_index("grid")):
            copy.wait()

        def filled(slot, j, row, count):
            start = pl.multiple_of(j * width, width)
            lines = []
            for b in range(row, row + count, BLOCK):
                tiles = []
                for c in range(0, width, BLOCK):
                    fill = fill_ref[0, j * (width // BLOCK) + c // BLOCK, b // BLOCK].astype(jnp.float32)
                    tiles.append(sums[slot, b - row : b - row + BLOCK, pl.ds(start + c, BLOCK)] * -fill)
                lines.append(tiles[0] if len(tiles) == 1 else jnp.concatenate(tiles, 1))
            return lines[0] if len(lines) == 1 else jnp.concatenate(lines, 0)

        for r in range(0, rows, step):
            here, slot = slice(r, r + step), r // step % 2
            sums[slot] = begun_ref[here, :] + jnp.dot(
                l_ref[here, done:], u_all[...], preferred_element_type=jnp.float32
            )
            if r < WS:
                for j in range(layers):
                    low = filled(slot, j, r, step).astype(jnp.bfloat16)
                    for g in range(step // piece_rows):
                        pivot_ref[j, r // piece_rows + g] = low[g * piece_rows : (g + 1) * piece_rows]
            for i in range(layers // 2):
                keep_ref[i, here, :] = filled(slot, 2 * i + core, r, step)
                send_ref[i, here, :] = filled(slot, 2 * i + 1 - core, r, step).astype(jnp.bfloat16)

    return kernel_call(
        body,
        (
            jax.ShapeDtypeStruct((layers // 2, rows, width), jnp.float32),
            jax.ShapeDtypeStruct((layers // 2, rows, width), jnp.bfloat16),
            jax.ShapeDtypeStruct((layers, grids, piece_rows, width), jnp.bfloat16),
        ),
        [SMEM, VMEM, VMEM] + [HBM] * len(pieces),
        scratch=[
            pltpu.VMEM((depth, columns), jnp.bfloat16),
            pltpu.VMEM((2, step, columns), jnp.float32),
            pltpu.SemaphoreType.DMA((len(pieces), panels)),
        ],
        flops=2 * rows * depth * columns,
        nbytes=2 * rows * depth + 2 * depth * columns + 8 * rows * columns,
    )(copy_fill, begun, masked, *pieces.values())


def tree(layers):
    nodes, level = [], 0
    while 2 << level <= layers:
        size = 2 << level
        for j in range(layers // size):
            low = j * size
            below = [n for n, first, span, _ in nodes if low <= first < low + size]
            nodes.append((layers - (layers >> level) + j, low, size, below))
        level += 1
    return nodes


def pick_pivots(candidates, sep_owner, grids, after):
    layers, _, piece_rows, width = candidates.shape
    nodes = tree(layers)

    def body(owner_ref, c_ref, *refs):
        out_ref = refs[-1]
        for node, low, size, _ in nodes:
            owner = owner_ref[node]
            total = c_ref[low, owner].astype(jnp.float32)
            for i in range(low + 1, low + size):
                total = total + c_ref[i, owner].astype(jnp.float32)
            total = total.astype(jnp.bfloat16)
            for g in range(grids):
                out_ref[g, node] = total

    return kernel_call(
        body,
        jax.ShapeDtypeStruct((grids, len(nodes), piece_rows, width), jnp.bfloat16),
        [SMEM, VMEM] + [ANY] * len(after),
        nbytes=4 * candidates.size,
    )(sep_owner, candidates, *after)


def eliminate(own, other, pivots, below, sep_panels):
    rows, width = own.shape
    grids, count, piece_rows, _ = pivots.shape
    nodes = tree(count + 1)
    inner = [n for n in nodes if n[3]]
    _, wide, part, _ = below[0].shape
    step = min(rows, 256)

    def body(own_ref, other_ref, p_ref, sep_ref, *refs):
        below_refs = refs[: len(below)]
        out_ref, all_p, all_below = refs[len(below) :]
        core = lax.rem(lax.axis_index("layer"), 2)
        for k, ref in enumerate(below_refs):
            at = pl.multiple_of((core ^ k) * part, part)
            for i in range(len(inner)):
                for m in inner[i][3]:
                    all_below[i, m, pl.ds(at, part), :] = ref[i, m]
        for node, _, _, under in nodes:
            at = node * WS
            for g in range(grids):
                all_p[at + g * piece_rows : at + (g + 1) * piece_rows, :] = p_ref[g, node]
            if under:
                which = [n[0] for n in inner].index(node)
                pivot = all_p[at : at + WS, :].astype(jnp.float32)
                for m in under:
                    pivot = pivot - jnp.dot(
                        all_below[which, m], all_p[m * WS : (m + 1) * WS, :], preferred_element_type=jnp.float32
                    )
                all_p[at : at + WS, :] = pivot.astype(jnp.bfloat16)
        for r in range(0, rows, step):
            here = slice(r, r + step)
            total = own_ref[here, :] + other_ref[here, :].astype(jnp.float32)
            for node in range(count):
                total = total - jnp.dot(
                    sep_ref[node, here, :], all_p[node * WS : (node + 1) * WS, :], preferred_element_type=jnp.float32
                )
            out_ref[here, :] = total

    return kernel_call(
        body,
        jax.ShapeDtypeStruct((rows, width), jnp.float32),
        [VMEM] * (4 + len(below)),
        scratch=[
            pltpu.VMEM((count * WS, width), jnp.bfloat16),
            pltpu.VMEM((len(inner), wide, WS, WS), jnp.bfloat16),
        ],
        flops=2 * rows * count * WS * width,
        nbytes=10 * rows * width + 2 * sep_panels.size,
    )(own, other, pivots, sep_panels, *below)


def local(l_panels, u_panels, panel_fill, copy_fill, sep_panels, sep_owner):
    layers, grids = lax.axis_size("layer"), lax.axis_size("grid")
    layer, me = lax.axis_index("layer"), lax.axis_index("grid")

    hops = masks(grids)
    far, near = hops[0], hops[-1]
    pieces = {0: u_panels}
    below = pick_below(sep_panels, sep_owner)
    beside = apart(u_panels, "grid", near)
    for hop in hops[:-1]:
        for k, piece in list(pieces.items()):
            pieces[k ^ hop] = apart(piece, "grid", hop)
    blocks = [k * u_panels.shape[2] // BLOCK for k in pieces]
    order = list(dict.fromkeys(blocks))
    masked = mask_panels(l_panels, jnp.swapaxes(panel_fill, 2, 3), order)
    below = below + apart(below, "grid", far)
    last = list(pieces)[-1]
    pieces[near] = beside
    for k in list(pieces)[1:-1]:
        if k == hops[1]:
            pieces[k], beside = together(pieces[k], beside)
        if k == last:
            pieces[k], below, masked = together(pieces[k], below, masked)
        pieces[k ^ near] = apart(pieces[k], "grid", near)
    for hop in hops[1:-1]:
        below = below + apart(below, "grid", hop)
    last ^= near
    pieces[last], below = together(pieces[last], below)

    half = len(order) - 1
    early = {k: piece for k, piece in pieces.items() if k * piece.shape[2] // BLOCK in order[:half]}
    late = {k: piece for k, piece in pieces.items() if k not in early}
    begun = first_part(masked, early, order)
    keep, send, candidates = layer_copy(begun, masked, late, order, grids, jnp.swapaxes(copy_fill, 1, 2))
    shape = candidates.shape
    candidates = lax.all_to_all(candidates.reshape((layers * grids,) + shape[2:]), BOTH, 0, 0).reshape(shape)

    below = [below + apart(below, "grid", hops[-1])]
    below.append(apart(below[0], "layer", 1))
    other = apart(send, "layer", 1)
    pivots = None
    bit = 1
    while keep.shape[0] > 1:
        bit *= 2
        half = keep.shape[0] // 2
        total = keep + other.astype(jnp.float32)
        total = total.reshape((half, 2) + total.shape[1:])
        side = (layer // bit) % 2
        keep = lax.dynamic_index_in_dim(total, side, 1, keepdims=False)
        send = lax.dynamic_index_in_dim(total, 1 - side, 1, keepdims=False).astype(jnp.bfloat16)
        if pivots is None:
            pivots = lax.all_to_all(pick_pivots(candidates, sep_owner, grids, [send, below[0]]), "grid", 0, 0)
        other = apart(send, "layer", bit)
    return eliminate(keep[0], other[0], pivots, below, sep_panels)


def solution(mesh):
    return jax.shard_map(
        local,
        mesh=mesh,
        in_specs=(
            P("layer", None, "grid", None),
            P("layer", None, "grid", None),
            P("layer", None, "grid", None),
            P("layer", "grid", None),
            P(None, "grid", None),
            P(),
        ),
        out_specs=P("grid", "layer"),
        check_vma=False,
    )
```

```python
import jax
import jax.numpy as jnp
from jax import lax
from jax.experimental import pallas as pl
from jax.experimental.pallas import tpu as pltpu
from jax.sharding import PartitionSpec as P

BLOCK = 128
WS = 256
VMEM_LIMIT = 40 << 20
EARLY_LIMIT = 60 << 20
BOTH = ("layer", "grid")
VMEM = pl.BlockSpec(memory_space=pltpu.VMEM)
HBM = pl.BlockSpec(memory_space=pltpu.HBM)
ANY = pl.BlockSpec(memory_space=pl.ANY)
SMEM = pl.BlockSpec(memory_space=pltpu.SMEM)


def kernel_call(body, out_shape, in_specs, scratch=(), flops=0, nbytes=0, limit=VMEM_LIMIT, out_specs=None):
    many = isinstance(out_shape, (tuple, list))
    return pl.pallas_call(
        body,
        out_shape=out_shape,
        in_specs=in_specs,
        out_specs=out_specs or ([VMEM] * len(out_shape) if many else VMEM),
        scratch_shapes=list(scratch),
        compiler_params=pltpu.CompilerParams(vmem_limit_bytes=limit),
        cost_estimate=pl.CostEstimate(flops=flops, bytes_accessed=nbytes, transcendentals=0),
    )


def apart(x, axis, distance):
    return lax.ppermute(x, axis, [(i, i ^ distance) for i in range(lax.axis_size(axis))])


def masks(count):
    top = count.bit_length() - 1
    return [3 << i - 1 for i in range(top - 1, 1, -1)] + [1 << i for i in (1, 0) if i < top]


def together(*xs):
    return lax.optimization_barrier(xs)


def pick_below(sep_panels, sep_owner):
    inner = [n for n in tree(lax.axis_size("layer")) if n[3]]
    wide = max(max(n[3]) for n in inner) + 1
    part = WS // 2

    def body(owner_ref, sep_ref, out_ref, held, owner, sems):
        start = pl.multiple_of(lax.rem(lax.axis_index("layer"), 2) * part, part)
        copies = [
            pltpu.make_async_copy(owner_ref, owner, sems.at[0]),
            pltpu.make_async_copy(sep_ref.at[:wide, pl.ds(start, part)], held, sems.at[1]),
        ]
        for copy in copies:
            copy.start()
        for copy in copies:
            copy.wait()
        for i, n in enumerate(inner):
            mine = owner[n[0]] == lax.axis_index("grid")
            out_ref[i] = jnp.where(mine, held[...], jnp.zeros(held.shape, held.dtype))

    return kernel_call(
        body,
        jax.ShapeDtypeStruct((len(inner), wide, part, WS), jnp.bfloat16),
        [HBM, HBM],
        scratch=[
            pltpu.VMEM((wide, part, WS), jnp.bfloat16),
            pltpu.SMEM(sep_owner.shape, jnp.int32),
            pltpu.SemaphoreType.DMA((2,)),
        ],
        nbytes=4 * wide * part * WS,
        limit=EARLY_LIMIT,
    )(sep_owner, sep_panels)


def mask_panels(l_panels, panel_fill, order):
    _, panels, rows, width = l_panels.shape
    share = width // lax.axis_size("grid")
    step = min(rows, 256)

    def body(panel_ref, l_ref, out_ref, l_all, fill_ref, sems, sem):
        first = lax.axis_index("grid") * share // BLOCK
        copies = [
            pltpu.make_async_copy(l_ref.at[0, :, r : r + step], l_all.at[:, r : r + step], sems.at[r // step])
            for r in range(0, rows, step)
        ]
        fill_copy = pltpu.make_async_copy(panel_ref, fill_ref, sem)
        fill_copy.start()
        for copy in copies:
            copy.start()
        fill_copy.wait()
        for r in range(0, rows, step):
            copies[r // step].wait()
            for i, block in enumerate(order):
                j = first ^ block
                for k in range(panels):
                    at = (i * panels + k) * BLOCK
                    for b in range(r, r + step, BLOCK):
                        here = fill_ref[0, k, j, b // BLOCK] != 0
                        tile = l_all[k, b : b + BLOCK, pl.ds(pl.multiple_of(j * BLOCK, BLOCK), BLOCK)]
                        out_ref[b : b + BLOCK, at : at + BLOCK] = jnp.where(here, tile, jnp.zeros_like(tile))

    return kernel_call(
        body,
        jax.ShapeDtypeStruct((rows, panels * width), jnp.bfloat16),
        [HBM, HBM],
        scratch=[
            pltpu.VMEM((panels, rows, width), jnp.bfloat16),
            pltpu.SMEM(panel_fill.shape, jnp.int32),
            pltpu.SemaphoreType.DMA((rows // step,)),
            pltpu.SemaphoreType.DMA,
        ],
        nbytes=4 * panels * rows * width,
    )(*(pltpu.with_memory_space_constraint(x, pltpu.HBM) for x in (panel_fill, l_panels)))


def load_panels(u_refs, pieces, order, u_all, sems, me):
    _, panels, share, _ = u_refs[0].shape
    copies = []
    for i, (k, ref) in enumerate(zip(pieces, u_refs)):
        block, inside = order.index(k * share // BLOCK), (me ^ k) * share % BLOCK
        for p in range(panels):
            at = pl.multiple_of((block * panels + p) * BLOCK + inside, share)
            copies.append(pltpu.make_async_copy(ref.at[0, p], u_all.at[pl.ds(at, share), :], sems.at[i, p]))
            copies[-1].start()
    return copies


def first_part(masked, pieces, order):
    rows, _ = masked.shape
    _, panels, share, columns = pieces[0].shape
    depth = panels * share * len(pieces)
    step = min(rows, 256)

    def body(l_ref, *refs):
        u_refs, (out_ref, u_all, sems) = refs[: len(pieces)], refs[len(pieces) :]
        for copy in load_panels(u_refs, list(pieces), order, u_all, sems, lax.axis_index("grid")):
            copy.wait()
        for r in range(0, rows, step):
            here = slice(r, r + step)
            out_ref[here, :] = jnp.dot(l_ref[here, :depth], u_all[...], preferred_element_type=jnp.float32)

    return kernel_call(
        body,
        jax.ShapeDtypeStruct((rows, columns), jnp.float32),
        [VMEM] + [HBM] * len(pieces),
        scratch=[pltpu.VMEM((depth, columns), jnp.bfloat16), pltpu.SemaphoreType.DMA((len(pieces), panels))],
        flops=2 * rows * depth * columns,
        nbytes=2 * rows * depth + 2 * depth * columns + 4 * rows * columns,
    )(masked, *pieces.values())


def layer_copy(begun, masked, pieces, order, grids, copy_fill):
    rows, columns = begun.shape
    panels, share = next(iter(pieces.values())).shape[1:3]
    layers = lax.axis_size("layer")
    width = columns // layers
    piece_rows = WS // grids
    step = min(rows, 256)
    depth = panels * share * len(pieces)
    done = masked.shape[1] - depth

    def body(fill_ref, begun_ref, l_ref, *refs):
        u_refs = refs[: len(pieces)]
        keep_ref, send_ref, pivot_ref, u_all, sums, fills, pivots, sems, sem = refs[len(pieces) :]
        core = lax.rem(lax.axis_index("layer"), 2)
        copies = load_panels(
            u_refs, list(pieces), order[-(depth // panels // BLOCK) :], u_all, sems, lax.axis_index("grid")
        )
        for b in range(rows // BLOCK):
            for c in range(columns // BLOCK):
                fill = -fill_ref[0, c, b].astype(jnp.float32)
                fills[b : b + 1, c * BLOCK : (c + 1) * BLOCK] = jnp.full((1, BLOCK), fill, jnp.float32)
        for copy in copies:
            copy.wait()

        def filled(slot, j, row, count):
            at = pl.ds(pl.multiple_of(j * width, width), width)
            lines = [
                sums[slot, b - row : b - row + BLOCK, at] * fills[b // BLOCK : b // BLOCK + 1, at]
                for b in range(row, row + count, BLOCK)
            ]
            return lines[0] if len(lines) == 1 else jnp.concatenate(lines, 0)

        out = pltpu.make_async_copy(pivots, pivot_ref, sem)
        for r in range(0, rows, step):
            here, slot = slice(r, r + step), r // step % 2
            sums[slot] = begun_ref[here, :] + jnp.dot(
                l_ref[here, done:], u_all[...], preferred_element_type=jnp.float32
            )
            if r < WS:
                for j in range(layers):
                    low = filled(slot, j, r, step).astype(jnp.bfloat16)
                    for g in range(step // piece_rows):
                        pivots[j, r // piece_rows + g] = low[g * piece_rows : (g + 1) * piece_rows]
            if r + step == WS:
                out.start()
            for i in range(layers // 2):
                keep_ref[i, here, :] = filled(slot, 2 * i + core, r, step)
                send_ref[i, here, :] = filled(slot, 2 * i + 1 - core, r, step).astype(jnp.bfloat16)
        out.wait()

    return kernel_call(
        body,
        (
            jax.ShapeDtypeStruct((layers // 2, rows, width), jnp.float32),
            jax.ShapeDtypeStruct((layers // 2, rows, width), jnp.bfloat16),
            jax.ShapeDtypeStruct((layers, grids, piece_rows, width), jnp.bfloat16),
        ),
        [SMEM, VMEM, VMEM] + [HBM] * len(pieces),
        out_specs=[VMEM, VMEM, HBM],
        scratch=[
            pltpu.VMEM((depth, columns), jnp.bfloat16),
            pltpu.VMEM((2, step, columns), jnp.float32),
            pltpu.VMEM((rows // BLOCK, columns), jnp.float32),
            pltpu.VMEM((layers, grids, piece_rows, width), jnp.bfloat16),
            pltpu.SemaphoreType.DMA((len(pieces), panels)),
            pltpu.SemaphoreType.DMA,
        ],
        flops=2 * rows * depth * columns,
        nbytes=2 * rows * depth + 2 * depth * columns + 8 * rows * columns,
    )(copy_fill, begun, masked, *pieces.values())


def tree(layers):
    nodes, level = [], 0
    while 2 << level <= layers:
        size = 2 << level
        for j in range(layers // size):
            low = j * size
            below = [n for n, first, span, _ in nodes if low <= first < low + size]
            nodes.append((layers - (layers >> level) + j, low, size, below))
        level += 1
    return nodes


def pick_pivots(candidates, sep_owner, grids, after):
    layers, _, piece_rows, width = candidates.shape
    nodes = tree(layers)

    def body(owner_ref, c_ref, *refs):
        out_ref = refs[-1]
        for node, low, size, _ in nodes:
            owner = owner_ref[node]
            total = c_ref[low, owner].astype(jnp.float32)
            for i in range(low + 1, low + size):
                total = total + c_ref[i, owner].astype(jnp.float32)
            total = total.astype(jnp.bfloat16)
            for g in range(grids):
                out_ref[g, node] = total

    return kernel_call(
        body,
        jax.ShapeDtypeStruct((grids, len(nodes), piece_rows, width), jnp.bfloat16),
        [SMEM, VMEM] + [ANY] * len(after),
        nbytes=4 * candidates.size,
    )(sep_owner, candidates, *after)


def eliminate(own, other, pivots, below, sep_panels):
    rows, width = own.shape
    grids, count, piece_rows, _ = pivots.shape
    nodes = tree(count + 1)
    inner = [n for n in nodes if n[3]]
    _, wide, part, _ = below[0].shape
    step = min(rows, 256)

    def body(own_ref, other_ref, p_ref, sep_ref, *refs):
        below_refs = refs[: len(below)]
        out_ref, all_p, all_below, result, sems = refs[len(below) :]
        core = lax.rem(lax.axis_index("layer"), 2)
        for k, ref in enumerate(below_refs):
            at = pl.multiple_of((core ^ k) * part, part)
            for i in range(len(inner)):
                for m in inner[i][3]:
                    all_below[i, m, pl.ds(at, part), :] = ref[i, m]
        for node, _, _, under in nodes:
            at = node * WS
            for g in range(grids):
                all_p[at + g * piece_rows : at + (g + 1) * piece_rows, :] = p_ref[g, node]
            if under:
                which = [n[0] for n in inner].index(node)
                pivot = all_p[at : at + WS, :].astype(jnp.float32)
                for m in under:
                    pivot = pivot - jnp.dot(
                        all_below[which, m], all_p[m * WS : (m + 1) * WS, :], preferred_element_type=jnp.float32
                    )
                all_p[at : at + WS, :] = pivot.astype(jnp.bfloat16)
        copies = []
        for r in range(0, rows, step):
            here = slice(r, r + step)
            total = own_ref[here, :] + other_ref[here, :].astype(jnp.float32)
            for node in range(count):
                total = total - jnp.dot(
                    sep_ref[node, here, :], all_p[node * WS : (node + 1) * WS, :], preferred_element_type=jnp.float32
                )
            result[here, :] = total
            copies.append(pltpu.make_async_copy(result.at[here], out_ref.at[here], sems.at[r // step]))
            copies[-1].start()
        for copy in copies:
            copy.wait()

    return kernel_call(
        body,
        jax.ShapeDtypeStruct((rows, width), jnp.float32),
        [VMEM] * (4 + len(below)),
        scratch=[
            pltpu.VMEM((count * WS, width), jnp.bfloat16),
            pltpu.VMEM((len(inner), wide, WS, WS), jnp.bfloat16),
            pltpu.VMEM((rows, width), jnp.float32),
            pltpu.SemaphoreType.DMA((rows // step,)),
        ],
        out_specs=HBM,
        flops=2 * rows * count * WS * width,
        nbytes=10 * rows * width + 2 * sep_panels.size,
    )(own, other, pivots, sep_panels, *below)


def local(l_panels, u_panels, panel_fill, copy_fill, sep_panels, sep_owner):
    layers, grids = lax.axis_size("layer"), lax.axis_size("grid")
    layer, me = lax.axis_index("layer"), lax.axis_index("grid")

    hops = masks(grids)
    far, near = hops[0], hops[-1]
    pieces = {0: u_panels}
    below = pick_below(sep_panels, sep_owner)
    beside = apart(u_panels, "grid", near)
    for hop in hops[:-1]:
        for k, piece in list(pieces.items()):
            pieces[k ^ hop] = apart(piece, "grid", hop)
    blocks = [k * u_panels.shape[2] // BLOCK for k in pieces]
    order = list(dict.fromkeys(blocks))
    masked = mask_panels(l_panels, jnp.swapaxes(panel_fill, 2, 3), order)
    below = below + apart(below, "grid", far)
    last = list(pieces)[-1]
    pieces[near] = beside
    for k in list(pieces)[1:-1]:
        if k == hops[1]:
            pieces[k], beside = together(pieces[k], beside)
        if k == last:
            pieces[k], below, masked = together(pieces[k], below, masked)
        pieces[k ^ near] = apart(pieces[k], "grid", near)
    for hop in hops[1:-1]:
        below = below + apart(below, "grid", hop)
    last ^= near
    pieces[last], below = together(pieces[last], below)

    half = len(order) - 1
    early = {k: piece for k, piece in pieces.items() if k * piece.shape[2] // BLOCK in order[:half]}
    late = {k: piece for k, piece in pieces.items() if k not in early}
    begun = first_part(masked, early, order)
    keep, send, candidates = layer_copy(begun, masked, late, order, grids, jnp.swapaxes(copy_fill, 1, 2))
    shape = candidates.shape
    candidates = lax.all_to_all(candidates.reshape((layers * grids,) + shape[2:]), BOTH, 0, 0).reshape(shape)

    below = [below + apart(below, "grid", hops[-1])]
    below.append(apart(below[0], "layer", 1))
    other = apart(send, "layer", 1)
    pivots = None
    bit = 1
    while keep.shape[0] > 1:
        bit *= 2
        half = keep.shape[0] // 2
        total = keep + other.astype(jnp.float32)
        total = total.reshape((half, 2) + total.shape[1:])
        side = (layer // bit) % 2
        keep = lax.dynamic_index_in_dim(total, side, 1, keepdims=False)
        send = lax.dynamic_index_in_dim(total, 1 - side, 1, keepdims=False).astype(jnp.bfloat16)
        if pivots is None:
            pivots = lax.all_to_all(pick_pivots(candidates, sep_owner, grids, [send, below[0]]), "grid", 0, 0)
        other = apart(send, "layer", bit)
    return eliminate(keep[0], other[0], pivots, below, sep_panels)


def solution(mesh):
    return jax.shard_map(
        local,
        mesh=mesh,
        in_specs=(
            P("layer", None, "grid", None),
            P("layer", None, "grid", None),
            P("layer", None, "grid", None),
            P("layer", "grid", None),
            P(None, "grid", None),
            P(),
        ),
        out_specs=P("grid", "layer"),
        check_vma=False,
    )
```

```python
import jax
import jax.numpy as jnp
from jax import lax
from jax.experimental import pallas as pl
from jax.experimental.pallas import tpu as pltpu
from jax.sharding import PartitionSpec as P

BLOCK = 128
WS = 256
VMEM_LIMIT = 40 << 20
EARLY_LIMIT = 60 << 20
BOTH = ("layer", "grid")
VMEM = pl.BlockSpec(memory_space=pltpu.VMEM)
HBM = pl.BlockSpec(memory_space=pltpu.HBM)
ANY = pl.BlockSpec(memory_space=pl.ANY)
SMEM = pl.BlockSpec(memory_space=pltpu.SMEM)


def kernel_call(body, out_shape, in_specs, scratch=(), flops=0, nbytes=0, limit=VMEM_LIMIT, out_specs=None):
    many = isinstance(out_shape, (tuple, list))
    return pl.pallas_call(
        body,
        out_shape=out_shape,
        in_specs=in_specs,
        out_specs=out_specs or ([VMEM] * len(out_shape) if many else VMEM),
        scratch_shapes=list(scratch),
        compiler_params=pltpu.CompilerParams(vmem_limit_bytes=limit),
        cost_estimate=pl.CostEstimate(flops=flops, bytes_accessed=nbytes, transcendentals=0),
    )


def apart(x, axis, distance):
    return lax.ppermute(x, axis, [(i, i ^ distance) for i in range(lax.axis_size(axis))])


def masks(count):
    top = count.bit_length() - 1
    return [3 << i - 1 for i in range(top - 1, 1, -1)] + [1 << i for i in (1, 0) if i < top]


def together(*xs):
    return lax.optimization_barrier(xs)


def pick_below(sep_panels, sep_owner):
    inner = [n for n in tree(lax.axis_size("layer")) if n[3]]
    wide = max(max(n[3]) for n in inner) + 1
    part = WS // 2

    def body(owner_ref, sep_ref, out_ref, held, owner, sems):
        start = pl.multiple_of(lax.rem(lax.axis_index("layer"), 2) * part, part)
        copies = [
            pltpu.make_async_copy(owner_ref, owner, sems.at[0]),
            pltpu.make_async_copy(sep_ref.at[:wide, pl.ds(start, part)], held, sems.at[1]),
        ]
        for copy in copies:
            copy.start()
        for copy in copies:
            copy.wait()
        for i, n in enumerate(inner):
            mine = owner[n[0]] == lax.axis_index("grid")
            out_ref[i] = jnp.where(mine, held[...], jnp.zeros(held.shape, held.dtype))

    return kernel_call(
        body,
        jax.ShapeDtypeStruct((len(inner), wide, part, WS), jnp.bfloat16),
        [HBM, HBM],
        scratch=[
            pltpu.VMEM((wide, part, WS), jnp.bfloat16),
            pltpu.SMEM(sep_owner.shape, jnp.int32),
            pltpu.SemaphoreType.DMA((2,)),
        ],
        nbytes=4 * wide * part * WS,
        limit=EARLY_LIMIT,
    )(sep_owner, sep_panels)


def mask_panels(l_panels, panel_fill, order):
    _, panels, rows, width = l_panels.shape
    share = width // lax.axis_size("grid")
    step = min(rows, 256)

    def body(panel_ref, l_ref, out_ref, l_all, fill_ref, sems, sem):
        first = lax.axis_index("grid") * share // BLOCK
        copies = [
            pltpu.make_async_copy(l_ref.at[0, :, r : r + step], l_all.at[:, r : r + step], sems.at[r // step])
            for r in range(0, rows, step)
        ]
        fill_copy = pltpu.make_async_copy(panel_ref, fill_ref, sem)
        fill_copy.start()
        for copy in copies:
            copy.start()
        fill_copy.wait()
        for r in range(0, rows, step):
            copies[r // step].wait()
            for i, block in enumerate(order):
                j = first ^ block
                for k in range(panels):
                    at = (i * panels + k) * BLOCK
                    for b in range(r, r + step, BLOCK):
                        here = fill_ref[0, k, j, b // BLOCK] != 0
                        tile = l_all[k, b : b + BLOCK, pl.ds(pl.multiple_of(j * BLOCK, BLOCK), BLOCK)]
                        out_ref[b : b + BLOCK, at : at + BLOCK] = jnp.where(here, tile, jnp.zeros_like(tile))

    return kernel_call(
        body,
        jax.ShapeDtypeStruct((rows, panels * width), jnp.bfloat16),
        [HBM, HBM],
        scratch=[
            pltpu.VMEM((panels, rows, width), jnp.bfloat16),
            pltpu.SMEM(panel_fill.shape, jnp.int32),
            pltpu.SemaphoreType.DMA((rows // step,)),
            pltpu.SemaphoreType.DMA,
        ],
        nbytes=4 * panels * rows * width,
    )(*(pltpu.with_memory_space_constraint(x, pltpu.HBM) for x in (panel_fill, l_panels)))


def load_panels(u_refs, pieces, order, u_all, sems, me):
    _, panels, share, _ = u_refs[0].shape
    copies = []
    for i, (k, ref) in enumerate(zip(pieces, u_refs)):
        block, inside = order.index(k * share // BLOCK), (me ^ k) * share % BLOCK
        for p in range(panels):
            at = pl.multiple_of((block * panels + p) * BLOCK + inside, share)
            copies.append(pltpu.make_async_copy(ref.at[0, p], u_all.at[pl.ds(at, share), :], sems.at[i, p]))
            copies[-1].start()
    return copies


def first_part(masked, pieces, order):
    rows, _ = masked.shape
    _, panels, share, columns = pieces[0].shape
    depth = panels * share * len(pieces)
    step = min(rows, 256)

    def body(l_ref, *refs):
        u_refs, (out_ref, u_all, sems) = refs[: len(pieces)], refs[len(pieces) :]
        for copy in load_panels(u_refs, list(pieces), order, u_all, sems, lax.axis_index("grid")):
            copy.wait()
        for r in range(0, rows, step):
            here = slice(r, r + step)
            out_ref[here, :] = jnp.dot(l_ref[here, :depth], u_all[...], preferred_element_type=jnp.float32)

    return kernel_call(
        body,
        jax.ShapeDtypeStruct((rows, columns), jnp.float32),
        [VMEM] + [HBM] * len(pieces),
        scratch=[pltpu.VMEM((depth, columns), jnp.bfloat16), pltpu.SemaphoreType.DMA((len(pieces), panels))],
        flops=2 * rows * depth * columns,
        nbytes=2 * rows * depth + 2 * depth * columns + 4 * rows * columns,
    )(masked, *pieces.values())


def layer_copy(begun, masked, pieces, order, copy_fill):
    rows, columns = begun.shape
    panels, share = next(iter(pieces.values())).shape[1:3]
    layers = lax.axis_size("layer")
    width = columns // layers
    step = min(rows, 256)
    depth = panels * share * len(pieces)
    done = masked.shape[1] - depth

    def body(fill_ref, begun_ref, l_ref, *refs):
        u_refs = refs[: len(pieces)]
        keep_ref, send_ref, top_ref, u_all, sums, fills, sems = refs[len(pieces) :]
        core = lax.rem(lax.axis_index("layer"), 2)
        copies = load_panels(
            u_refs, list(pieces), order[-(depth // panels // BLOCK) :], u_all, sems, lax.axis_index("grid")
        )
        for b in range(rows // BLOCK):
            for c in range(columns // BLOCK):
                fill = -fill_ref[0, c, b].astype(jnp.float32)
                fills[b : b + 1, c * BLOCK : (c + 1) * BLOCK] = jnp.full((1, BLOCK), fill, jnp.float32)
        for copy in copies:
            copy.wait()

        def filled(slot, j, row, count):
            at = pl.ds(pl.multiple_of(j * width, width), width)
            lines = [
                sums[slot, b - row : b - row + BLOCK, at] * fills[b // BLOCK : b // BLOCK + 1, at]
                for b in range(row, row + count, BLOCK)
            ]
            return lines[0] if len(lines) == 1 else jnp.concatenate(lines, 0)

        for r in range(0, rows, step):
            here, slot = slice(r, r + step), r // step % 2
            sums[slot] = begun_ref[here, :] + jnp.dot(
                l_ref[here, done:], u_all[...], preferred_element_type=jnp.float32
            )
            for i in range(layers // 2):
                keep_ref[i, here, :] = filled(slot, 2 * i + core, r, step)
                other = filled(slot, 2 * i + 1 - core, r, step)
                send_ref[i, here, :] = other.astype(jnp.bfloat16)
                if r < WS:
                    top_ref[i, here, :] = other

    return kernel_call(
        body,
        (
            jax.ShapeDtypeStruct((layers // 2, rows, width), jnp.float32),
            jax.ShapeDtypeStruct((layers // 2, rows, width), jnp.bfloat16),
            jax.ShapeDtypeStruct((layers // 2, WS, width), jnp.float32),
        ),
        [SMEM, VMEM, VMEM] + [HBM] * len(pieces),
        scratch=[
            pltpu.VMEM((depth, columns), jnp.bfloat16),
            pltpu.VMEM((2, step, columns), jnp.float32),
            pltpu.VMEM((rows // BLOCK, columns), jnp.float32),
            pltpu.SemaphoreType.DMA((len(pieces), panels)),
        ],
        flops=2 * rows * depth * columns,
        nbytes=2 * rows * depth + 2 * depth * columns + 8 * rows * columns,
    )(copy_fill, begun, masked, *pieces.values())


def tree(layers):
    nodes, level = [], 0
    while 2 << level <= layers:
        size = 2 << level
        for j in range(layers // size):
            low = j * size
            below = [n for n, first, span, _ in nodes if low <= first < low + size]
            nodes.append((layers - (layers >> level) + j, low, size, below))
        level += 1
    return nodes


def pick_pivots(candidates, sep_owner, grids, after):
    pairs, _, piece_rows, width = candidates.shape
    nodes = tree(2 * pairs)

    def body(owner_ref, c_ref, *refs):
        out_ref = refs[-1]
        for node, low, size, _ in nodes:
            owner = owner_ref[node]
            total = c_ref[low // 2, owner].astype(jnp.float32)
            for i in range(low // 2 + 1, (low + size) // 2):
                total = total + c_ref[i, owner].astype(jnp.float32)
            total = total.astype(jnp.bfloat16)
            for g in range(grids):
                out_ref[g, node] = total

    return kernel_call(
        body,
        jax.ShapeDtypeStruct((grids, len(nodes), piece_rows, width), jnp.bfloat16),
        [SMEM, VMEM] + [ANY] * len(after),
        nbytes=4 * candidates.size,
    )(sep_owner, candidates, *after)


def eliminate(own, other, pivots, below, sep_panels):
    rows, width = own.shape
    grids, count, piece_rows, _ = pivots.shape
    nodes = tree(count + 1)
    inner = [n for n in nodes if n[3]]
    _, wide, part, _ = below[0].shape
    step = min(rows, 256)

    def body(own_ref, other_ref, p_ref, sep_ref, *refs):
        below_refs = refs[: len(below)]
        out_ref, all_p, all_below, result, sems = refs[len(below) :]
        core = lax.rem(lax.axis_index("layer"), 2)
        for k, ref in enumerate(below_refs):
            at = pl.multiple_of((core ^ k) * part, part)
            for i in range(len(inner)):
                for m in inner[i][3]:
                    all_below[i, m, pl.ds(at, part), :] = ref[i, m]
        for node, _, _, under in nodes:
            at = node * WS
            for g in range(grids):
                all_p[at + g * piece_rows : at + (g + 1) * piece_rows, :] = p_ref[g, node]
            if under:
                which = [n[0] for n in inner].index(node)
                pivot = all_p[at : at + WS, :].astype(jnp.float32)
                for m in under:
                    pivot = pivot - jnp.dot(
                        all_below[which, m], all_p[m * WS : (m + 1) * WS, :], preferred_element_type=jnp.float32
                    )
                all_p[at : at + WS, :] = pivot.astype(jnp.bfloat16)
        copies = []
        for r in range(0, rows, step):
            here = slice(r, r + step)
            total = own_ref[here, :] + other_ref[here, :].astype(jnp.float32)
            for node in range(count):
                total = total - jnp.dot(
                    sep_ref[node, here, :], all_p[node * WS : (node + 1) * WS, :], preferred_element_type=jnp.float32
                )
            result[here, :] = total
            copies.append(pltpu.make_async_copy(result.at[here], out_ref.at[here], sems.at[r // step]))
            copies[-1].start()
        for copy in copies:
            copy.wait()

    return kernel_call(
        body,
        jax.ShapeDtypeStruct((rows, width), jnp.float32),
        [VMEM] * (4 + len(below)),
        scratch=[
            pltpu.VMEM((count * WS, width), jnp.bfloat16),
            pltpu.VMEM((len(inner), wide, WS, WS), jnp.bfloat16),
            pltpu.VMEM((rows, width), jnp.float32),
            pltpu.SemaphoreType.DMA((rows // step,)),
        ],
        out_specs=HBM,
        flops=2 * rows * count * WS * width,
        nbytes=10 * rows * width + 2 * sep_panels.size,
    )(own, other, pivots, sep_panels, *below)


def local(l_panels, u_panels, panel_fill, copy_fill, sep_panels, sep_owner):
    layers, grids = lax.axis_size("layer"), lax.axis_size("grid")
    layer, me = lax.axis_index("layer"), lax.axis_index("grid")

    hops = masks(grids)
    far, near = hops[0], hops[-1]
    pieces = {0: u_panels}
    below = pick_below(sep_panels, sep_owner)
    beside = apart(u_panels, "grid", near)
    for hop in hops[:-1]:
        for k, piece in list(pieces.items()):
            pieces[k ^ hop] = apart(piece, "grid", hop)
    blocks = [k * u_panels.shape[2] // BLOCK for k in pieces]
    order = list(dict.fromkeys(blocks))
    masked = mask_panels(l_panels, jnp.swapaxes(panel_fill, 2, 3), order)
    below = below + apart(below, "grid", far)
    last = list(pieces)[-1]
    pieces[near] = beside
    for k in list(pieces)[1:-1]:
        if k == hops[1]:
            pieces[k], beside = together(pieces[k], beside)
        if k == last:
            pieces[k], below, masked = together(pieces[k], below, masked)
        pieces[k ^ near] = apart(pieces[k], "grid", near)
    for hop in hops[1:-1]:
        below = below + apart(below, "grid", hop)
    last ^= near
    pieces[last], below = together(pieces[last], below)

    half = len(order) - 1
    early = {k: piece for k, piece in pieces.items() if k * piece.shape[2] // BLOCK in order[:half]}
    late = {k: piece for k, piece in pieces.items() if k not in early}
    begun = first_part(masked, early, order)
    keep, send, top = layer_copy(begun, masked, late, order, jnp.swapaxes(copy_fill, 1, 2))
    candidates = (keep[:, :WS] + apart(top, "layer", 1)).astype(jnp.bfloat16)
    candidates = candidates.reshape((layers // 2 * grids, WS // grids) + candidates.shape[2:])
    alike = [[i * grids + g for i in range(core, layers, 2) for g in range(grids)] for core in (0, 1)]
    candidates, send, below = together(candidates, send, below)
    candidates = lax.all_to_all(candidates, BOTH, 0, 0, axis_index_groups=alike)
    candidates = candidates.reshape((layers // 2, grids) + candidates.shape[1:])

    below = [below + apart(below, "grid", hops[-1])]
    below.append(apart(below[0], "layer", 1))
    other = apart(send, "layer", 1)
    pivots = None
    bit = 1
    while keep.shape[0] > 1:
        bit *= 2
        half = keep.shape[0] // 2
        total = keep + other.astype(jnp.float32)
        total = total.reshape((half, 2) + total.shape[1:])
        side = (layer // bit) % 2
        keep = lax.dynamic_index_in_dim(total, side, 1, keepdims=False)
        send = lax.dynamic_index_in_dim(total, 1 - side, 1, keepdims=False).astype(jnp.bfloat16)
        if pivots is None:
            pivots = lax.all_to_all(pick_pivots(candidates, sep_owner, grids, [send]), "grid", 0, 0)
        other = apart(send, "layer", bit)
    return eliminate(keep[0], other[0], pivots, below, sep_panels)


def solution(mesh):
    return jax.shard_map(
        local,
        mesh=mesh,
        in_specs=(
            P("layer", None, "grid", None),
            P("layer", None, "grid", None),
            P("layer", None, "grid", None),
            P("layer", "grid", None),
            P(None, "grid", None),
            P(),
        ),
        out_specs=P("grid", "layer"),
        check_vma=False,
    )
```

```python
import jax
import jax.numpy as jnp
from jax import lax
from jax.experimental import pallas as pl
from jax.experimental.pallas import tpu as pltpu
from jax.sharding import PartitionSpec as P

BLOCK = 128
WS = 256
VMEM_LIMIT = 40 << 20
EARLY_LIMIT = 60 << 20
BOTH = ("layer", "grid")
VMEM = pl.BlockSpec(memory_space=pltpu.VMEM)
HBM = pl.BlockSpec(memory_space=pltpu.HBM)
ANY = pl.BlockSpec(memory_space=pl.ANY)
SMEM = pl.BlockSpec(memory_space=pltpu.SMEM)


def kernel_call(body, out_shape, in_specs, scratch=(), flops=0, nbytes=0, limit=VMEM_LIMIT, out_specs=None):
    many = isinstance(out_shape, (tuple, list))
    return pl.pallas_call(
        body,
        out_shape=out_shape,
        in_specs=in_specs,
        out_specs=out_specs or ([VMEM] * len(out_shape) if many else VMEM),
        scratch_shapes=list(scratch),
        compiler_params=pltpu.CompilerParams(vmem_limit_bytes=limit),
        cost_estimate=pl.CostEstimate(flops=flops, bytes_accessed=nbytes, transcendentals=0),
    )


def apart(x, axis, distance):
    return lax.ppermute(x, axis, [(i, i ^ distance) for i in range(lax.axis_size(axis))])


def masks(count):
    top = count.bit_length() - 1
    return [3 << i - 1 for i in range(top - 1, 1, -1)] + [1 << i for i in (1, 0) if i < top]


def together(*xs):
    return lax.optimization_barrier(xs)


def pick_below(sep_panels, sep_owner):
    inner = [n for n in tree(lax.axis_size("layer")) if n[3]]
    wide = max(max(n[3]) for n in inner) + 1
    part = WS // 2

    def body(owner_ref, sep_ref, out_ref, held, owner, sems):
        start = pl.multiple_of(lax.rem(lax.axis_index("layer"), 2) * part, part)
        copies = [
            pltpu.make_async_copy(owner_ref, owner, sems.at[0]),
            pltpu.make_async_copy(sep_ref.at[:wide, pl.ds(start, part)], held, sems.at[1]),
        ]
        for copy in copies:
            copy.start()
        for copy in copies:
            copy.wait()
        for i, n in enumerate(inner):
            mine = owner[n[0]] == lax.axis_index("grid")
            out_ref[i] = jnp.where(mine, held[...], jnp.zeros(held.shape, held.dtype))

    return kernel_call(
        body,
        jax.ShapeDtypeStruct((len(inner), wide, part, WS), jnp.bfloat16),
        [HBM, HBM],
        scratch=[
            pltpu.VMEM((wide, part, WS), jnp.bfloat16),
            pltpu.SMEM(sep_owner.shape, jnp.int32),
            pltpu.SemaphoreType.DMA((2,)),
        ],
        nbytes=4 * wide * part * WS,
        limit=EARLY_LIMIT,
    )(sep_owner, sep_panels)


def mask_panels(l_panels, panel_fill, order):
    _, panels, rows, width = l_panels.shape
    share = width // lax.axis_size("grid")
    step = min(rows, 256)

    def body(panel_ref, l_ref, out_ref, l_all, fill_ref, sems, sem):
        first = lax.axis_index("grid") * share // BLOCK
        copies = [
            pltpu.make_async_copy(l_ref.at[0, :, r : r + step], l_all.at[:, r : r + step], sems.at[r // step])
            for r in range(0, rows, step)
        ]
        fill_copy = pltpu.make_async_copy(panel_ref, fill_ref, sem)
        fill_copy.start()
        for copy in copies:
            copy.start()
        fill_copy.wait()
        for r in range(0, rows, step):
            copies[r // step].wait()
            for i, block in enumerate(order):
                j = first ^ block
                for k in range(panels):
                    at = (i * panels + k) * BLOCK
                    for b in range(r, r + step, BLOCK):
                        here = fill_ref[0, k, j, b // BLOCK] != 0
                        tile = l_all[k, b : b + BLOCK, pl.ds(pl.multiple_of(j * BLOCK, BLOCK), BLOCK)]
                        out_ref[b : b + BLOCK, at : at + BLOCK] = jnp.where(here, tile, jnp.zeros_like(tile))

    return kernel_call(
        body,
        jax.ShapeDtypeStruct((rows, panels * width), jnp.bfloat16),
        [HBM, HBM],
        scratch=[
            pltpu.VMEM((panels, rows, width), jnp.bfloat16),
            pltpu.SMEM(panel_fill.shape, jnp.int32),
            pltpu.SemaphoreType.DMA((rows // step,)),
            pltpu.SemaphoreType.DMA,
        ],
        nbytes=4 * panels * rows * width,
    )(*(pltpu.with_memory_space_constraint(x, pltpu.HBM) for x in (panel_fill, l_panels)))


def load_panels(u_refs, pieces, order, u_all, sems, me):
    _, panels, share, _ = u_refs[0].shape
    copies = []
    for i, (k, ref) in enumerate(zip(pieces, u_refs)):
        block, inside = order.index(k * share // BLOCK), (me ^ k) * share % BLOCK
        for p in range(panels):
            at = pl.multiple_of((block * panels + p) * BLOCK + inside, share)
            copies.append(pltpu.make_async_copy(ref.at[0, p], u_all.at[pl.ds(at, share), :], sems.at[i, p]))
            copies[-1].start()
    return copies


def first_part(masked, pieces, order):
    rows, _ = masked.shape
    _, panels, share, columns = pieces[0].shape
    depth = panels * share * len(pieces)
    step = min(rows, 256)

    def body(l_ref, *refs):
        u_refs, (out_ref, u_all, sems) = refs[: len(pieces)], refs[len(pieces) :]
        for copy in load_panels(u_refs, list(pieces), order, u_all, sems, lax.axis_index("grid")):
            copy.wait()
        for r in range(0, rows, step):
            here = slice(r, r + step)
            out_ref[here, :] = jnp.dot(l_ref[here, :depth], u_all[...], preferred_element_type=jnp.float32)

    return kernel_call(
        body,
        jax.ShapeDtypeStruct((rows, columns), jnp.float32),
        [VMEM] + [HBM] * len(pieces),
        scratch=[pltpu.VMEM((depth, columns), jnp.bfloat16), pltpu.SemaphoreType.DMA((len(pieces), panels))],
        flops=2 * rows * depth * columns,
        nbytes=2 * rows * depth + 2 * depth * columns + 4 * rows * columns,
    )(masked, *pieces.values())


def layer_copy(begun, masked, pieces, order, copy_fill):
    rows, columns = begun.shape
    panels, share = next(iter(pieces.values())).shape[1:3]
    layers = lax.axis_size("layer")
    width = columns // layers
    step = min(rows, 256)
    depth = panels * share * len(pieces)
    done = masked.shape[1] - depth

    def body(fill_ref, begun_ref, l_ref, *refs):
        u_refs = refs[: len(pieces)]
        keep_ref, send_ref, top_ref, u_all, sums, fills, sems = refs[len(pieces) :]
        core = lax.rem(lax.axis_index("layer"), 2)
        copies = load_panels(
            u_refs, list(pieces), order[-(depth // panels // BLOCK) :], u_all, sems, lax.axis_index("grid")
        )
        for b in range(rows // BLOCK):
            for c in range(columns // BLOCK):
                fill = -fill_ref[0, c, b].astype(jnp.float32)
                fills[b : b + 1, c * BLOCK : (c + 1) * BLOCK] = jnp.full((1, BLOCK), fill, jnp.float32)
        for copy in copies:
            copy.wait()

        def filled(slot, j, row, count):
            at = pl.ds(pl.multiple_of(j * width, width), width)
            lines = [
                sums[slot, b - row : b - row + BLOCK, at] * fills[b // BLOCK : b // BLOCK + 1, at]
                for b in range(row, row + count, BLOCK)
            ]
            return lines[0] if len(lines) == 1 else jnp.concatenate(lines, 0)

        for r in range(0, rows, step):
            here, slot = slice(r, r + step), r // step % 2
            sums[slot] = begun_ref[here, :] + jnp.dot(
                l_ref[here, done:], u_all[...], preferred_element_type=jnp.float32
            )
            for i in range(layers // 2):
                keep_ref[i, here, :] = filled(slot, 2 * i + core, r, step)
                other = filled(slot, 2 * i + 1 - core, r, step)
                send_ref[i, here, :] = other.astype(jnp.bfloat16)
                if r < WS:
                    top_ref[i, here, :] = other

    return kernel_call(
        body,
        (
            jax.ShapeDtypeStruct((layers // 2, rows, width), jnp.float32),
            jax.ShapeDtypeStruct((layers // 2, rows, width), jnp.bfloat16),
            jax.ShapeDtypeStruct((layers // 2, WS, width), jnp.float32),
        ),
        [SMEM, VMEM, VMEM] + [HBM] * len(pieces),
        scratch=[
            pltpu.VMEM((depth, columns), jnp.bfloat16),
            pltpu.VMEM((2, step, columns), jnp.float32),
            pltpu.VMEM((rows // BLOCK, columns), jnp.float32),
            pltpu.SemaphoreType.DMA((len(pieces), panels)),
        ],
        flops=2 * rows * depth * columns,
        nbytes=2 * rows * depth + 2 * depth * columns + 8 * rows * columns,
    )(copy_fill, begun, masked, *pieces.values())


def tree(layers):
    nodes, level = [], 0
    while 2 << level <= layers:
        size = 2 << level
        for j in range(layers // size):
            low = j * size
            below = [n for n, first, span, _ in nodes if low <= first < low + size]
            nodes.append((layers - (layers >> level) + j, low, size, below))
        level += 1
    return nodes


def pick_pivots(candidates, sep_owner, grids, after):
    pairs, _, piece_rows, width = candidates.shape
    nodes = tree(2 * pairs)

    def body(owner_ref, c_ref, *refs):
        out_ref = refs[-1]
        for node, low, size, _ in nodes:
            owner = owner_ref[node]
            total = c_ref[low // 2, owner].astype(jnp.float32)
            for i in range(low // 2 + 1, (low + size) // 2):
                total = total + c_ref[i, owner].astype(jnp.float32)
            total = total.astype(jnp.bfloat16)
            for g in range(grids):
                out_ref[g, node] = total

    return kernel_call(
        body,
        jax.ShapeDtypeStruct((grids, len(nodes), piece_rows, width), jnp.bfloat16),
        [SMEM, VMEM] + [ANY] * len(after),
        nbytes=4 * candidates.size,
    )(sep_owner, candidates, *after)


def eliminate(own, other, pivots, below, sep_panels):
    rows, width = own.shape
    grids, count, piece_rows, _ = pivots.shape
    nodes = tree(count + 1)
    inner = [n for n in nodes if n[3]]
    _, wide, part, _ = below[0].shape
    step = min(rows, 256)

    def body(own_ref, other_ref, p_ref, sep_ref, *refs):
        below_refs = refs[: len(below)]
        out_ref, all_p, all_below, result, sems = refs[len(below) :]
        core = lax.rem(lax.axis_index("layer"), 2)
        for k, ref in enumerate(below_refs):
            at = pl.multiple_of((core ^ k) * part, part)
            for i in range(len(inner)):
                for m in inner[i][3]:
                    all_below[i, m, pl.ds(at, part), :] = ref[i, m]
        for node, _, _, under in nodes:
            at = node * WS
            for g in range(grids):
                all_p[at + g * piece_rows : at + (g + 1) * piece_rows, :] = p_ref[g, node]
            if under:
                which = [n[0] for n in inner].index(node)
                pivot = all_p[at : at + WS, :].astype(jnp.float32)
                taken = jnp.zeros_like(pivot)
                for m in under:
                    taken = taken + jnp.dot(
                        all_below[which, m], all_p[m * WS : (m + 1) * WS, :], preferred_element_type=jnp.float32
                    )
                all_p[at : at + WS, :] = (pivot - taken).astype(jnp.bfloat16)
        copies = []
        for r in range(0, rows, step):
            here = slice(r, r + step)
            total = own_ref[here, :] + other_ref[here, :].astype(jnp.float32)
            taken = jnp.zeros_like(total)
            for node in range(count):
                taken = taken + jnp.dot(
                    sep_ref[node, here, :], all_p[node * WS : (node + 1) * WS, :], preferred_element_type=jnp.float32
                )
            result[here, :] = total - taken
            copies.append(pltpu.make_async_copy(result.at[here], out_ref.at[here], sems.at[r // step]))
            copies[-1].start()
        for copy in copies:
            copy.wait()

    return kernel_call(
        body,
        jax.ShapeDtypeStruct((rows, width), jnp.float32),
        [VMEM] * (4 + len(below)),
        scratch=[
            pltpu.VMEM((count * WS, width), jnp.bfloat16),
            pltpu.VMEM((len(inner), wide, WS, WS), jnp.bfloat16),
            pltpu.VMEM((rows, width), jnp.float32),
            pltpu.SemaphoreType.DMA((rows // step,)),
        ],
        out_specs=HBM,
        flops=2 * rows * count * WS * width,
        nbytes=10 * rows * width + 2 * sep_panels.size,
    )(own, other, pivots, sep_panels, *below)


def local(l_panels, u_panels, panel_fill, copy_fill, sep_panels, sep_owner):
    layers, grids = lax.axis_size("layer"), lax.axis_size("grid")
    layer, me = lax.axis_index("layer"), lax.axis_index("grid")

    hops = masks(grids)
    far, near = hops[0], hops[-1]
    pieces = {0: u_panels}
    below = pick_below(sep_panels, sep_owner)
    beside = apart(u_panels, "grid", near)
    for hop in hops[:-1]:
        for k, piece in list(pieces.items()):
            if k == far:
                piece, _ = together(piece, below)
            pieces[k ^ hop] = apart(piece, "grid", hop)
    blocks = [k * u_panels.shape[2] // BLOCK for k in pieces]
    order = list(dict.fromkeys(blocks))
    masked = mask_panels(l_panels, jnp.swapaxes(panel_fill, 2, 3), order)
    below = below + apart(below, "grid", far)
    last = list(pieces)[-1]
    pieces[near] = beside
    for k in list(pieces)[1:-1]:
        if k == hops[1]:
            pieces[k], beside = together(pieces[k], beside)
        if k == last:
            pieces[k], below, masked = together(pieces[k], below, masked)
        pieces[k ^ near] = apart(pieces[k], "grid", near)
    for hop in hops[1:-1]:
        below = below + apart(below, "grid", hop)
    last ^= near
    pieces[last], below = together(pieces[last], below)

    half = len(order) - 1
    early = {k: piece for k, piece in pieces.items() if k * piece.shape[2] // BLOCK in order[:half]}
    late = {k: piece for k, piece in pieces.items() if k not in early}
    begun = first_part(masked, early, order)
    keep, send, top = layer_copy(begun, masked, late, order, jnp.swapaxes(copy_fill, 1, 2))
    candidates = (keep[:, :WS] + apart(top, "layer", 1)).astype(jnp.bfloat16)
    candidates = candidates.reshape((layers // 2 * grids, WS // grids) + candidates.shape[2:])
    alike = [[i * grids + g for i in range(core, layers, 2) for g in range(grids)] for core in (0, 1)]
    candidates, send, below = together(candidates, send, below)
    candidates = lax.all_to_all(candidates, BOTH, 0, 0, axis_index_groups=alike)
    candidates = candidates.reshape((layers // 2, grids) + candidates.shape[1:])

    below = [below + apart(below, "grid", hops[-1])]
    below.append(apart(below[0], "layer", 1))
    other = apart(send, "layer", 1)
    pivots = None
    bit = 1
    while keep.shape[0] > 1:
        bit *= 2
        half = keep.shape[0] // 2
        total = keep + other.astype(jnp.float32)
        total = total.reshape((half, 2) + total.shape[1:])
        side = (layer // bit) % 2
        keep = lax.dynamic_index_in_dim(total, side, 1, keepdims=False)
        send = lax.dynamic_index_in_dim(total, 1 - side, 1, keepdims=False).astype(jnp.bfloat16)
        if pivots is None:
            pivots = lax.all_to_all(pick_pivots(candidates, sep_owner, grids, [send]), "grid", 0, 0)
        other = apart(send, "layer", bit)
    return eliminate(keep[0], other[0], pivots, below, sep_panels)


def solution(mesh):
    return jax.shard_map(
        local,
        mesh=mesh,
        in_specs=(
            P("layer", None, "grid", None),
            P("layer", None, "grid", None),
            P("layer", None, "grid", None),
            P("layer", "grid", None),
            P(None, "grid", None),
            P(),
        ),
        out_specs=P("grid", "layer"),
        check_vma=False,
    )
```

```python
import functools

import jax
import jax.numpy as jnp
from jax import lax
from jax.experimental import pallas as pl
from jax.experimental.pallas import tpu as pltpu
from jax.sharding import PartitionSpec as P

BLOCK = 128
WS = 256
VMEM_LIMIT = 40 << 20
EARLY_LIMIT = 60 << 20
BOTH = ("layer", "grid")
VMEM = pl.BlockSpec(memory_space=pltpu.VMEM)
HBM = pl.BlockSpec(memory_space=pltpu.HBM)
ANY = pl.BlockSpec(memory_space=pl.ANY)
SMEM = pl.BlockSpec(memory_space=pltpu.SMEM)


def kernel_call(body, out_shape, in_specs, scratch=(), flops=0, nbytes=0, limit=VMEM_LIMIT, out_specs=None):
    many = isinstance(out_shape, (tuple, list))
    return pl.pallas_call(
        body,
        out_shape=out_shape,
        in_specs=in_specs,
        out_specs=out_specs or ([VMEM] * len(out_shape) if many else VMEM),
        scratch_shapes=list(scratch),
        compiler_params=pltpu.CompilerParams(vmem_limit_bytes=limit),
        cost_estimate=pl.CostEstimate(flops=flops, bytes_accessed=nbytes, transcendentals=0),
    )


def apart(x, axis, distance):
    return lax.ppermute(x, axis, [(i, i ^ distance) for i in range(lax.axis_size(axis))])


def masks(count):
    top = count.bit_length() - 1
    return [3 << i - 1 for i in range(top - 1, 1, -1)] + [1 << i for i in (1, 0) if i < top]


def together(*xs):
    return lax.optimization_barrier(xs)


def pick_below(sep_panels, sep_owner):
    inner = [n for n in tree(lax.axis_size("layer")) if n[3]]
    wide = max(max(n[3]) for n in inner) + 1
    part = WS // 2

    def body(owner_ref, sep_ref, out_ref, held, owner, sems):
        start = pl.multiple_of(lax.rem(lax.axis_index("layer"), 2) * part, part)
        copies = [
            pltpu.make_async_copy(owner_ref, owner, sems.at[0]),
            pltpu.make_async_copy(sep_ref.at[:wide, pl.ds(start, part)], held, sems.at[1]),
        ]
        for copy in copies:
            copy.start()
        for copy in copies:
            copy.wait()
        for i, n in enumerate(inner):
            mine = owner[n[0]] == lax.axis_index("grid")
            out_ref[i] = jnp.where(mine, held[...], jnp.zeros(held.shape, held.dtype))

    return kernel_call(
        body,
        jax.ShapeDtypeStruct((len(inner), wide, part, WS), jnp.bfloat16),
        [HBM, HBM],
        scratch=[
            pltpu.VMEM((wide, part, WS), jnp.bfloat16),
            pltpu.SMEM(sep_owner.shape, jnp.int32),
            pltpu.SemaphoreType.DMA((2,)),
        ],
        nbytes=4 * wide * part * WS,
        limit=EARLY_LIMIT,
    )(sep_owner, sep_panels)


def mask_panels(l_panels, panel_fill, order):
    _, panels, rows, width = l_panels.shape
    share = width // lax.axis_size("grid")
    step = min(rows, 256)

    def body(panel_ref, l_ref, out_ref, l_all, fill_ref, sems, sem):
        first = lax.axis_index("grid") * share // BLOCK
        copies = [
            pltpu.make_async_copy(l_ref.at[0, :, r : r + step], l_all.at[:, r : r + step], sems.at[r // step])
            for r in range(0, rows, step)
        ]
        fill_copy = pltpu.make_async_copy(panel_ref, fill_ref, sem)
        fill_copy.start()
        for copy in copies:
            copy.start()
        fill_copy.wait()
        for r in range(0, rows, step):
            copies[r // step].wait()
            for i, block in enumerate(order):
                j = first ^ block
                for k in range(panels):
                    at = (i * panels + k) * BLOCK
                    for b in range(r, r + step, BLOCK):
                        here = fill_ref[0, k, j, b // BLOCK] != 0
                        tile = l_all[k, b : b + BLOCK, pl.ds(pl.multiple_of(j * BLOCK, BLOCK), BLOCK)]
                        out_ref[b : b + BLOCK, at : at + BLOCK] = jnp.where(here, tile, jnp.zeros_like(tile))

    return kernel_call(
        body,
        jax.ShapeDtypeStruct((rows, panels * width), jnp.bfloat16),
        [HBM, HBM],
        scratch=[
            pltpu.VMEM((panels, rows, width), jnp.bfloat16),
            pltpu.SMEM(panel_fill.shape, jnp.int32),
            pltpu.SemaphoreType.DMA((rows // step,)),
            pltpu.SemaphoreType.DMA,
        ],
        nbytes=4 * panels * rows * width,
    )(*(pltpu.with_memory_space_constraint(x, pltpu.HBM) for x in (panel_fill, l_panels)))


def load_panels(u_refs, pieces, order, u_all, sems, me):
    _, panels, share, _ = u_refs[0].shape
    copies = []
    for i, (k, ref) in enumerate(zip(pieces, u_refs)):
        block, inside = order.index(k * share // BLOCK), (me ^ k) * share % BLOCK
        for p in range(panels):
            at = pl.multiple_of((block * panels + p) * BLOCK + inside, share)
            copies.append(pltpu.make_async_copy(ref.at[0, p], u_all.at[pl.ds(at, share), :], sems.at[i, p]))
            copies[-1].start()
    return copies


def first_part(masked, pieces, order):
    rows, _ = masked.shape
    _, panels, share, columns = pieces[0].shape
    depth = panels * share * len(pieces)
    step = min(rows, 256)

    def body(l_ref, *refs):
        u_refs, (out_ref, u_all, sems) = refs[: len(pieces)], refs[len(pieces) :]
        for copy in load_panels(u_refs, list(pieces), order, u_all, sems, lax.axis_index("grid")):
            copy.wait()
        for r in range(0, rows, step):
            here = slice(r, r + step)
            out_ref[here, :] = jnp.dot(l_ref[here, :depth], u_all[...], preferred_element_type=jnp.float32)

    return kernel_call(
        body,
        jax.ShapeDtypeStruct((rows, columns), jnp.float32),
        [VMEM] + [HBM] * len(pieces),
        scratch=[pltpu.VMEM((depth, columns), jnp.bfloat16), pltpu.SemaphoreType.DMA((len(pieces), panels))],
        flops=2 * rows * depth * columns,
        nbytes=2 * rows * depth + 2 * depth * columns + 4 * rows * columns,
    )(masked, *pieces.values())


def layer_copy(begun, masked, pieces, order, grids, copy_fill):
    rows, columns = begun.shape
    panels, share = next(iter(pieces.values())).shape[1:3]
    layers = lax.axis_size("layer")
    width = columns // layers
    step = min(rows, 256)
    depth = panels * share * len(pieces)
    done = masked.shape[1] - depth

    def body(fill_ref, begun_ref, l_ref, *refs):
        u_refs = refs[: len(pieces)]
        keep_refs, send_refs = refs[len(pieces) :][: layers // 2], refs[len(pieces) :][layers // 2 : layers]
        top_ref, top_send_ref, u_all, sums, fills, sems = refs[len(pieces) + layers :]
        pair, core = lax.axis_index("layer") // 2, lax.rem(lax.axis_index("layer"), 2)
        copies = load_panels(
            u_refs, list(pieces), order[-(depth // panels // BLOCK) :], u_all, sems, lax.axis_index("grid")
        )
        for b in range(rows // BLOCK):
            for c in range(columns // BLOCK):
                fill = -fill_ref[0, c, b].astype(jnp.float32)
                fills[b : b + 1, c * BLOCK : (c + 1) * BLOCK] = jnp.full((1, BLOCK), fill, jnp.float32)
        for copy in copies:
            copy.wait()

        def filled(slot, j, row, count):
            at = pl.ds(pl.multiple_of(j * width, width), width)
            lines = [
                sums[slot, b - row : b - row + BLOCK, at] * fills[b // BLOCK : b // BLOCK + 1, at]
                for b in range(row, row + count, BLOCK)
            ]
            return lines[0] if len(lines) == 1 else jnp.concatenate(lines, 0)

        for r in range(0, rows, step):
            here, slot = slice(r, r + step), r // step % 2
            sums[slot] = begun_ref[here, :] + jnp.dot(
                l_ref[here, done:], u_all[...], preferred_element_type=jnp.float32
            )
            if r < WS:
                for i in range(layers // 2):
                    top_ref[i, here, :] = filled(slot, 2 * i + core, r, step)
                    top_send_ref[i, here, :] = filled(slot, 2 * i + 1 - core, r, step)
            for i in range(layers // 2):
                keep_refs[i][here, :] = filled(slot, 2 * (pair ^ i) + core, r, step)
                send_refs[i][here, :] = filled(slot, 2 * (pair ^ i) + 1 - core, r, step).astype(jnp.bfloat16)

    *blocks, top, top_send = kernel_call(
        body,
        [jax.ShapeDtypeStruct((rows, width), jnp.float32)] * (layers // 2)
        + [jax.ShapeDtypeStruct((rows, width), jnp.bfloat16)] * (layers // 2)
        + [jax.ShapeDtypeStruct((layers // 2, WS, width), jnp.float32)] * 2,
        [SMEM, VMEM, VMEM] + [HBM] * len(pieces),
        scratch=[
            pltpu.VMEM((depth, columns), jnp.bfloat16),
            pltpu.VMEM((2, step, columns), jnp.float32),
            pltpu.VMEM((rows // BLOCK, columns), jnp.float32),
            pltpu.SemaphoreType.DMA((len(pieces), panels)),
        ],
        flops=2 * rows * depth * columns,
        nbytes=2 * rows * depth + 2 * depth * columns + 8 * rows * columns,
    )(copy_fill, begun, masked, *pieces.values())
    return blocks[: layers // 2], blocks[layers // 2 :], top, top_send


def tree(layers):
    nodes, level = [], 0
    while 2 << level <= layers:
        size = 2 << level
        for j in range(layers // size):
            low = j * size
            below = [n for n, first, span, _ in nodes if low <= first < low + size]
            nodes.append((layers - (layers >> level) + j, low, size, below))
        level += 1
    return nodes


def pick_pivots(candidates, sep_owner, grids, after):
    pairs, _, piece_rows, width = candidates.shape
    nodes = tree(2 * pairs)

    def body(owner_ref, c_ref, *refs):
        out_ref = refs[-1]
        for node, low, size, _ in nodes:
            owner = owner_ref[node]
            total = c_ref[low // 2, owner].astype(jnp.float32)
            for i in range(low // 2 + 1, (low + size) // 2):
                total = total + c_ref[i, owner].astype(jnp.float32)
            total = total.astype(jnp.bfloat16)
            for g in range(grids):
                out_ref[g, node] = total

    return kernel_call(
        body,
        jax.ShapeDtypeStruct((grids, len(nodes), piece_rows, width), jnp.bfloat16),
        [SMEM, VMEM] + [ANY] * len(after),
        nbytes=4 * candidates.size,
    )(sep_owner, candidates, *after)


def eliminate(parts, pivots, below, sep_panels):
    rows, width = parts[0].shape
    grids, count, piece_rows, _ = pivots.shape
    nodes = tree(count + 1)
    inner = [n for n in nodes if n[3]]
    _, wide, part, _ = below[0].shape
    step = min(rows, 256)

    def body(p_ref, sep_ref, *refs):
        below_refs, refs = refs[: len(below)], refs[len(below) :]
        part_refs, refs = refs[: len(parts)], refs[len(parts) :]
        out_ref, all_p, all_below, result, sems = refs
        core = lax.rem(lax.axis_index("layer"), 2)
        for k, ref in enumerate(below_refs):
            at = pl.multiple_of((core ^ k) * part, part)
            for i in range(len(inner)):
                for m in inner[i][3]:
                    all_below[i, m, pl.ds(at, part), :] = ref[i, m]
        for node, _, _, under in nodes:
            at = node * WS
            for g in range(grids):
                all_p[at + g * piece_rows : at + (g + 1) * piece_rows, :] = p_ref[g, node]
            if under:
                which = [n[0] for n in inner].index(node)
                pivot = all_p[at : at + WS, :].astype(jnp.float32)
                for m in under:
                    pivot = pivot - jnp.dot(
                        all_below[which, m], all_p[m * WS : (m + 1) * WS, :], preferred_element_type=jnp.float32
                    )
                all_p[at : at + WS, :] = pivot.astype(jnp.bfloat16)
        copies = []
        for r in range(0, rows, step):
            here = slice(r, r + step)
            total = functools.reduce(jnp.add, [ref[here, :].astype(jnp.float32) for ref in part_refs])
            for node in range(count):
                total = total - jnp.dot(
                    sep_ref[node, here, :], all_p[node * WS : (node + 1) * WS, :], preferred_element_type=jnp.float32
                )
            result[here, :] = total
            copies.append(pltpu.make_async_copy(result.at[here], out_ref.at[here], sems.at[r // step]))
            copies[-1].start()
        for copy in copies:
            copy.wait()

    return kernel_call(
        body,
        jax.ShapeDtypeStruct((rows, width), jnp.float32),
        [VMEM] * (2 + len(below) + len(parts)),
        scratch=[
            pltpu.VMEM((count * WS, width), jnp.bfloat16),
            pltpu.VMEM((len(inner), wide, WS, WS), jnp.bfloat16),
            pltpu.VMEM((rows, width), jnp.float32),
            pltpu.SemaphoreType.DMA((rows // step,)),
        ],
        out_specs=HBM,
        flops=2 * rows * count * WS * width,
        nbytes=10 * rows * width + 2 * sep_panels.size,
    )(pivots, sep_panels, *below, *parts)


def local(l_panels, u_panels, panel_fill, copy_fill, sep_panels, sep_owner):
    layers, grids = lax.axis_size("layer"), lax.axis_size("grid")
    layer, me = lax.axis_index("layer"), lax.axis_index("grid")

    hops = masks(grids)
    far, near = hops[0], hops[-1]
    pieces = {0: u_panels}
    below = pick_below(sep_panels, sep_owner)
    beside = apart(u_panels, "grid", near)
    for hop in hops[:-1]:
        for k, piece in list(pieces.items()):
            pieces[k ^ hop] = apart(piece, "grid", hop)
    blocks = [k * u_panels.shape[2] // BLOCK for k in pieces]
    order = list(dict.fromkeys(blocks))
    masked = mask_panels(l_panels, jnp.swapaxes(panel_fill, 2, 3), order)
    below = below + apart(below, "grid", far)
    last = list(pieces)[-1]
    pieces[near] = beside
    for k in list(pieces)[1:-1]:
        if k == hops[1]:
            pieces[k], beside = together(pieces[k], beside)
        if k == last:
            pieces[k], below, masked = together(pieces[k], below, masked)
        pieces[k ^ near] = apart(pieces[k], "grid", near)
    for hop in hops[1:-1]:
        below = below + apart(below, "grid", hop)
    last ^= near
    pieces[last], below = together(pieces[last], below)

    half = len(order) - 1
    early = {k: piece for k, piece in pieces.items() if k * piece.shape[2] // BLOCK in order[:half]}
    late = {k: piece for k, piece in pieces.items() if k not in early}
    begun = first_part(masked, early, order)
    keep, send, top, top_send = layer_copy(begun, masked, late, order, grids, jnp.swapaxes(copy_fill, 1, 2))
    candidates = (top + apart(top_send, "layer", 1)).astype(jnp.bfloat16)
    candidates, below, *send = together(candidates, below, *send)
    candidates = candidates.reshape((layers // 2 * grids, WS // grids) + candidates.shape[2:])
    alike = [[i * grids + g for i in range(core, layers, 2) for g in range(grids)] for core in (0, 1)]
    candidates = lax.all_to_all(candidates, BOTH, 0, 0, axis_index_groups=alike)
    candidates = candidates.reshape((layers // 2, grids) + candidates.shape[1:])

    below = [below + apart(below, "grid", hops[-1])]
    below.append(apart(below[0], "layer", 1))
    parts = [[kept, apart(sent, "layer", 1)] for kept, sent in zip(keep, send)]
    pivots = None
    while len(parts) > 1:
        half = len(parts) // 2
        sums = [functools.reduce(jnp.add, [x.astype(jnp.float32) for x in part]) for part in parts[half:]]
        sums = [x.astype(jnp.bfloat16) for x in sums]
        if pivots is None:
            parts[0] = [functools.reduce(jnp.add, [x.astype(jnp.float32) for x in parts[0]])]
            pivots = lax.all_to_all(
                pick_pivots(candidates, sep_owner, grids, [sums[0], parts[0][0]]), "grid", 0, 0
            )
        parts = [part + [apart(x, "layer", 2 * half)] for part, x in zip(parts, sums)]
    return eliminate(parts[0], pivots, below, sep_panels)


def solution(mesh):
    return jax.shard_map(
        local,
        mesh=mesh,
        in_specs=(
            P("layer", None, "grid", None),
            P("layer", None, "grid", None),
            P("layer", None, "grid", None),
            P("layer", "grid", None),
            P(None, "grid", None),
            P(),
        ),
        out_specs=P("grid", "layer"),
        check_vma=False,
    )
```
